32 devices in a mesh: groups: 2 (over y), rows: 8 (over z, x), cols: 2 (over core).
Axes of the slice: x: 2, y: 2, z: 4, core: 2. Of those that a mesh axis runs over, the one named last changes fastest.
Arguments:
- snapshots: float32 [16, 24, 16, 256], P(('groups', 'rows'), None, None, 'cols'), parts along dimension 0, as said below
- labels: int32 [16, 24, 16], P(('groups', 'rows')), parts along dimension 0, may hold values from 0 to 7
- conductivity: float32 [16], P('groups'), parts along dimension 0, may hold values from 0.2 to 5
- pairing: int32 [6, 4, 128], replicated, may hold values from 0 to 127, each once within a row
Outputs:
- rotated: float32 [16, 24, 16, 256], P(('groups', 'rows'), None, None, 'cols'), parts along dimension 0
- sigma: float32 [512], P(('groups', 'cols')), parts along dimension 0
The draws below stay inside these ranges and needn't reach their ends.
There are 2 independent parts, one for each index of `groups`. The reference program is written for one: setup_inputs(seed, part) draws one part's arguments, and reference() takes and returns one part's arrays. A program takes and returns all parts, laid end to end along the dimension named above; an argument that names none is the same for every part. Nothing has to cross between parts.
Inputs may be any that keep to these rules, and one draw needn't show every extreme that they name: `snapshots`: real-valued temperature deviations. `pairing`: each row along the last dimension is a permutation; entries 2 j and 2 j + 1 name the two columns of one plane rotation.
All inputs are finite; a program needn't handle non-finite values.
Results may differ from the reference program's by a relative error of at most 0.0003.
Values sent between devices are 32-bit elements; how exact they have to be, the bound alone decides.
No kernel may reach another device: no remote copies, remote signals or barrier semaphores. Data moves between devices by JAX's collectives and lax.ppermute only.
A program may use at most 64 MiB of HBM per device.

```python
import math
import jax
import jax.numpy as jnp
from jax import lax

BW = 64
NY = 24
PLANES = 16
REGIONS = 8
SWEEPS = 2
ISTEPS = 4
NX = 8
SNAPSHOTS = 256
MEETS = 6
N_COLS = 2


def draw_snapshots(key, part):
    subkeys = jax.random.split(key, 5)
    full_shape = (NX, NY, PLANES, SNAPSHOTS)
    half_log = 0.5 * math.log(10.0)
    cell_scale = jnp.exp(jax.random.uniform(subkeys[1], (NX, NY, PLANES, 1), jnp.float32, -half_log, half_log))
    column_scale = jnp.exp(jax.random.uniform(subkeys[2], (SNAPSHOTS,), jnp.float32, -half_log, half_log))
    common = jax.random.normal(subkeys[3], (NX, NY, PLANES, 1), jnp.float32)
    rough_part = jax.random.normal(subkeys[0], full_shape, jnp.float32)
    loading = jax.random.normal(subkeys[4], (SNAPSHOTS,), jnp.float32)
    return (rough_part * cell_scale * column_scale + 0.7 * common * loading).astype(jnp.float32)


def touch_ends(drawn, rng, smallest, high):
    place = [jax.random.randint(jax.random.fold_in(rng, axis), (), 0, length) for axis, length in enumerate(drawn.shape)]
    main_axis = drawn.shape.index(max(drawn.shape))
    next_to = place[:main_axis] + [(place[main_axis] + 1) % drawn.shape[main_axis]] + place[main_axis + 1:]
    return drawn.at[tuple(place)].set(smallest).at[tuple(next_to)].set(high)


def setup_inputs(seed: int = 0, part: int = 0) -> dict:
    seeds = jax.random.split(jax.random.key(seed), 5)
    own_keys = jax.random.split(jax.random.fold_in(seeds[4], part), 5)
    snapshots = draw_snapshots(jax.random.fold_in(jax.random.fold_in(seeds[4], part), 71), part)
    labels = touch_ends(jax.random.randint(own_keys[1], (NX, NY, PLANES), 0, REGIONS), jax.random.fold_in(own_keys[1], 1), 0, REGIONS - 1).astype(jnp.int32)
    conductivity = jnp.clip(jnp.exp(jax.random.uniform(own_keys[2], (REGIONS,), jnp.float32, math.log(0.2), math.log(5.0))), 0.2, 5.0)
    pairing = jax.vmap(lambda own: jax.random.permutation(own, 2 * BW))(jax.random.split(seeds[3], MEETS * ISTEPS)).reshape((MEETS, ISTEPS, 2 * BW)).astype(jnp.int32)
    return dict(snapshots=snapshots, labels=labels, conductivity=conductivity, pairing=pairing)


HIGHEST_PRECISION = lax.Precision.HIGHEST

def contract_rows(left, right):
    return lax.dot_general(left, right, (((0,), (0,)), ((), ())), precision=HIGHEST_PRECISION, preferred_element_type=jnp.float32)

def rotation_factor(gram_matrix, rounds_pairs):
    pair_width = gram_matrix.shape[0]
    column_ids = jnp.arange(pair_width, dtype=jnp.int32)
    accumulated = jnp.eye(pair_width, dtype=jnp.float32)
    for rotation_round in range(rounds_pairs.shape[0]):
        sel_first = (rounds_pairs[rotation_round, 0::2][:, None] == column_ids[None, :]).astype(jnp.float32)
        sel_second = (rounds_pairs[rotation_round, 1::2][:, None] == column_ids[None, :]).astype(jnp.float32)
        diagonal = jnp.diagonal(gram_matrix)
        g_first = jnp.dot(sel_first, diagonal, precision=HIGHEST_PRECISION)
        g_second = jnp.dot(sel_second, diagonal, precision=HIGHEST_PRECISION)
        coupling = lax.optimization_barrier(jnp.sum(jnp.dot(sel_first, gram_matrix, precision=HIGHEST_PRECISION) * sel_second, axis=1))
        spread = g_first - g_second
        radius = jnp.sqrt(spread * spread + 4.0 * coupling * coupling)
        tangent = -2.0 * coupling * jnp.sign(spread) / (jnp.abs(spread) + radius + 1e-06 * (g_first + g_second + 1.0))
        cosine = 1.0 / jnp.sqrt(1.0 + tangent * tangent)
        sine_term = cosine * tangent
        turn = contract_rows(sel_first * cosine[:, None], sel_first) + contract_rows(sel_second * cosine[:, None], sel_second)
        turn = turn + contract_rows(sel_first * sine_term[:, None], sel_second) - contract_rows(sel_second * sine_term[:, None], sel_first)
        gram_matrix = contract_rows(turn, jnp.dot(gram_matrix, turn, precision=HIGHEST_PRECISION))
        accumulated = jnp.dot(accumulated, turn, precision=HIGHEST_PRECISION)
    return (accumulated, gram_matrix)

def differences(values, axis_number):
    padding = [(0, 0)] * values.ndim
    padding[axis_number] = (1, 1)
    padded = jnp.pad(values, padding)
    length = values.shape[axis_number]
    upper_part = lax.slice_in_dim(padded, 2, length + 2, axis=axis_number)
    lower_part = lax.slice_in_dim(padded, 0, length, axis=axis_number)
    return 0.5 * (upper_part - lower_part)

def augment(values, labels, conductivity):
    region_ids = jnp.arange(conductivity.shape[0], dtype=jnp.int32)
    onehot = (labels[..., None] == region_ids).astype(jnp.float32)
    weight = jnp.sqrt(lax.optimization_barrier(jnp.sum(onehot * conductivity, axis=-1)))[..., None]
    return jnp.stack([values, weight * differences(values, 0), weight * differences(values, 1), weight * differences(values, 2)])

def reference(snapshots, labels, conductivity, pairing):
    augmented = augment(snapshots, labels, conductivity)
    flat_rows = augmented.reshape(-1, SNAPSHOTS)
    block_count = 2 * N_COLS
    blocks = [flat_rows[:, index * BW:(index + 1) * BW] for index in range(block_count)]
    norms = [None] * block_count
    upper_ids = [2 * index for index in range(N_COLS)]
    lower_ids = [2 * index + 1 for index in range(N_COLS)]
    meeting = 0
    for sweep_index in range(SWEEPS):
        for round_index in range(2 * N_COLS - 1):
            for device_index in range(N_COLS):
                first_id = upper_ids[device_index]
                second_id = lower_ids[device_index]
                pair_block = jnp.concatenate([blocks[first_id], blocks[second_id]], axis=1)
                gram_matrix = contract_rows(pair_block, pair_block)
                factor, rotated_gram = rotation_factor(gram_matrix, pairing[meeting])
                pair_block = jnp.dot(pair_block, factor, precision=HIGHEST_PRECISION)
                blocks[first_id] = pair_block[:, :BW]
                blocks[second_id] = pair_block[:, BW:]
                column_norms = jnp.sqrt(jnp.diagonal(rotated_gram))
                norms[first_id] = column_norms[:BW]
                norms[second_id] = column_norms[BW:]
            meeting += 1
            upper_ids, lower_ids = ([upper_ids[0], lower_ids[0]] + upper_ids[1:-1], lower_ids[1:] + [upper_ids[-1]])
    rotated = jnp.concatenate(blocks, axis=1).reshape(augmented.shape)[0]
    sigma = jnp.concatenate(norms)
    return (rotated, sigma)
```

```python
import functools

import jax
import jax.numpy as jnp
from jax import lax
from jax.experimental import pallas as pl
from jax.experimental.pallas import tpu as pltpu
from jax.sharding import PartitionSpec as P

HIGHEST = lax.Precision.HIGHEST
VMEM = pl.BlockSpec(memory_space=pltpu.VMEM)
SMEM = pl.BlockSpec(memory_space=pltpu.SMEM)


def dot(left, right, dims=((1,), (0,))):
    return lax.dot_general(
        left, right, (dims, ((), ())), precision=HIGHEST, preferred_element_type=jnp.float32
    )


def local_kernel(stride, own_ref, other_ref, coefs_ref, gram_ref, turned_ref):
    u = own_ref[...]
    rows = u.shape[0]
    coefs = jnp.concatenate([coefs_ref[g].T for g in range(coefs_ref.shape[0])], axis=0)
    applied = coefs[:, 0:1] * u
    for column, step in ((1, 2 * stride), (2, -2 * stride), (3, 2), (4, -2)):
        applied -= coefs[:, column : column + 1] * pltpu.roll(u, (-step) % rows, 0)
    width = u.shape[1]
    turned_ref[:width, :] = u.T
    turned_ref[width:, :] = other_ref[...].T
    gram_ref[...] = dot(turned_ref[...], applied)


def halo_kernel(side_ref, own_ref, halo_ref, coefs_ref, gram_ref, turned_ref, kept_ref, sent_ref):
    coefs = jnp.concatenate([coefs_ref[g].T for g in range(coefs_ref.shape[0])], axis=0)
    applied = coefs[:, 0:1] * own_ref[...] - coefs[:, 1:2] * halo_ref[...]
    gram = gram_ref[...] + dot(turned_ref[...], applied)
    width = own_ref.shape[1]
    half = width // 2
    first = side_ref[0] == 0
    own = gram[:width]
    cross = gram[width:]
    cross = 0.5 * jnp.where(first, cross.T, cross)
    kept_ref[:width, :] = 0.5 * (own + own.T)
    kept_ref[width:, :] = jnp.where(first, cross[:half], cross[half:])
    sent_ref[...] = jnp.where(first, cross[half:], cross[:half])


def lanes(values, index):
    return jnp.take_along_axis(
        values, jnp.broadcast_to(index, values.shape), axis=1, mode="promise_in_bounds"
    )


def rotation(diagonal, opposite, coupling, first):
    g_first = jnp.where(first, diagonal, opposite)
    g_second = jnp.where(first, opposite, diagonal)
    spread = g_first - g_second
    radius = jnp.sqrt(spread * spread + 4.0 * coupling * coupling)
    sign = jnp.where(spread > 0, 1.0, jnp.where(spread < 0, -1.0, 0.0))
    tangent = (
        -2.0 * coupling * sign / (jnp.abs(spread) + radius + 1e-06 * (g_first + g_second + 1.0))
    )
    cosine = 1.0 / jnp.sqrt(1.0 + tangent * tangent)
    sine = cosine * tangent
    return cosine[:1], jnp.where(first, -sine, sine)[:1]


def tournament_kernel(
    meets, turns, side_ref, mine_ref, theirs_ref, partner_ref, first_ref, own_ref, other_ref, rotated_ref, sigma_ref
):
    n = own_ref.shape[1]
    h = n // 2
    side = side_ref[0] == 0
    mine, theirs = mine_ref[...], theirs_ref[...]
    zero_side = jnp.where(side, mine, theirs)
    one_side = jnp.where(side, theirs, mine)
    cross = jnp.concatenate([zero_side[n:], one_side[n:]], axis=0)
    row = lax.broadcasted_iota(jnp.int32, (n, n), 0)
    col = lax.broadcasted_iota(jnp.int32, (n, n), 1)
    eye = row == col
    identity = jnp.where(eye, 1.0, 0.0)
    blank = jnp.zeros((n, h), jnp.float32)
    gram = jnp.concatenate(
        [
            jnp.concatenate([zero_side[:n], cross], axis=1),
            jnp.concatenate([cross.T, one_side[:n]], axis=1),
        ],
        axis=0,
    )
    total = None
    upper, lower = [0, 2], [1, 3]
    for meeting in range(meets):
        met = [gram[:n, :n], gram[n:, n:]]
        factor = [identity, identity]
        for turn in range(turns):
            index = meeting * turns + turn
            partner = partner_ref[index : index + 1, :]
            first = first_ref[index : index + 1, :] > 0
            paired = row == partner
            for d in range(2):
                held = met[d]
                diagonal = jnp.sum(jnp.where(eye, held, 0.0), axis=0, keepdims=True)
                coupling = jnp.sum(jnp.where(paired, held, 0.0), axis=0, keepdims=True)
                diagonal = jnp.broadcast_to(diagonal, (8, n))
                coupling = jnp.broadcast_to(coupling, (8, n))
                cosine, sine = rotation(diagonal, lanes(diagonal, partner), coupling, first)
                held = (held * cosine + lanes(held, partner) * sine).T
                met[d] = held * cosine + lanes(held, partner) * sine
                factor[d] = factor[d] * cosine + lanes(factor[d], partner) * sine
        blocks = {}
        for d in range(2):
            for block, part in ((upper[d], factor[d][:, :h]), (lower[d], factor[d][:, h:])):
                blocks[block] = jnp.concatenate([part, blank] if d == 0 else [blank, part], axis=0)
        if meeting == meets - 1:
            after = range(4)
            norms = {}
            for d in range(2):
                norm = jnp.sqrt(jnp.sum(jnp.where(eye, met[d], 0.0), axis=0, keepdims=True))
                norms[upper[d]], norms[lower[d]] = norm[:, :h], norm[:, h:]
        else:
            upper, lower = [upper[0], lower[0]], [lower[1], upper[1]]
            after = [upper[0], lower[0], upper[1], lower[1]]
        wide = jnp.concatenate([blocks[block] for block in after], axis=1)
        total = wide if total is None else dot(total, wide)
        if meeting < meets - 1:
            gram = dot(wide, dot(gram, wide), ((0,), (0,)))
    picked = jnp.where(side, total[:, :n], total[:, n:])
    near = jnp.where(side, picked[:n], picked[n:])
    far = jnp.where(side, picked[n:], picked[:n])
    rotated_ref[...] = dot(own_ref[...], near) + dot(other_ref[...], far)
    sigma_ref[...] = jnp.where(
        side,
        jnp.concatenate([norms[0], norms[1]], axis=1),
        jnp.concatenate([norms[2], norms[3]], axis=1),
    )


def partners(pairing):
    n = pairing.shape[-1]
    flat = pairing.reshape(-1, n)
    ids = jnp.arange(n, dtype=jnp.int32)
    opposite = flat.reshape(-1, n // 2, 2)[:, :, ::-1].reshape(-1, n)
    here = flat[:, :, None] == ids
    partner = jnp.sum(jnp.where(here, opposite[:, :, None], 0), axis=1)
    first = jnp.sum(jnp.where(here, (1 - (ids & 1))[None, :, None], 0), axis=1)
    return partner, first


def moved(values, dim, step):
    padding = [(0, 0)] * values.ndim
    padding[dim] = (0, step) if step > 0 else (-step, 0)
    start = max(step, 0)
    return lax.slice_in_dim(jnp.pad(values, padding), start, start + values.shape[dim], axis=dim)


def inside(shape, dim, step):
    place = lax.broadcasted_iota(jnp.int32, shape, dim) + step
    return ((place >= 0) & (place < shape[dim])).astype(jnp.float32)


def packed(arrays, width):
    flat = [array.reshape(-1, width) for array in arrays]
    flat += [jnp.zeros_like(flat[0])] * (8 - len(flat))
    return jnp.stack(flat, axis=1)


def shards(snapshots, labels, conductivity, pairing):
    planes, ny, nz, width = snapshots.shape
    cells = planes * ny * nz
    half = width // 2
    count = lax.axis_size("rows")
    own = snapshots.reshape(cells, width)
    halo = lax.ppermute(own, "rows", [(i + 2, i) for i in range(count - 2)])
    other = lax.ppermute(own, "cols", [(0, 1), (1, 0)])

    region_ids = jnp.arange(conductivity.shape[0], dtype=jnp.int32)
    squared = 0.25 * jnp.sum((labels[0][..., None] == region_ids) * conductivity, axis=-1)
    after = lax.ppermute(squared, "rows", [(i + 1, i) for i in range(count - 1)])
    before = lax.ppermute(squared, "rows", [(i, i + 1) for i in range(count - 1)])
    around = [moved(squared, dim, step) for dim in (0, 1) for step in (1, -1)]
    valid = [inside((ny, nz), dim, 2 * step) for dim in (0, 1) for step in (1, -1)]
    local_coefs = packed(
        [1.0 + sum(around)] + [value * keep for value, keep in zip(around, valid)], width
    )
    halo_coefs = packed([after + before, 2.0 * after], width)
    partner, first = partners(pairing)
    side = lax.axis_index("cols").astype(jnp.int32).reshape(1)

    gram, turned = pl.pallas_call(
        functools.partial(local_kernel, nz),
        out_shape=(
            jax.ShapeDtypeStruct((2 * width, width), jnp.float32),
            jax.ShapeDtypeStruct((2 * width, cells), jnp.float32),
        ),
        in_specs=[VMEM] * 3,
        out_specs=[VMEM] * 2,
        cost_estimate=pl.CostEstimate(flops=12 * cells * width * width, bytes_accessed=4 * 6 * cells * width, transcendentals=0),
    )(own, other, local_coefs)
    kept, sent = pl.pallas_call(
        halo_kernel,
        out_shape=(
            jax.ShapeDtypeStruct((width + half, width), jnp.float32),
            jax.ShapeDtypeStruct((half, width), jnp.float32),
        ),
        in_specs=[SMEM] + [VMEM] * 5,
        out_specs=[VMEM] * 2,
    )(side, own, halo, halo_coefs, gram, turned)
    received = lax.ppermute(sent, "cols", [(0, 1), (1, 0)])
    share = jnp.concatenate([kept[:width], kept[width:] + received], axis=0)
    apart = 1
    while apart < count:
        share = share + lax.ppermute(share, "rows", [(i, i ^ apart) for i in range(count)])
        apart *= 2
    theirs = lax.ppermute(share, "cols", [(0, 1), (1, 0)])
    rotated, sigma = pl.pallas_call(
        functools.partial(tournament_kernel, pairing.shape[0], pairing.shape[1]),
        out_shape=(
            jax.ShapeDtypeStruct((cells, width), jnp.float32),
            jax.ShapeDtypeStruct((1, width), jnp.float32),
        ),
        in_specs=[SMEM] + [VMEM] * 6,
        out_specs=[VMEM] * 2,
    )(side, share, theirs, partner, first, own, other)
    return rotated.reshape(snapshots.shape), sigma.reshape(width)


def solution(mesh):
    placed = (
        P(("groups", "rows"), None, None, "cols"),
        P(("groups", "rows"), None, None),
        P("groups"),
        P(),
    )
    return jax.shard_map(
        shards,
        mesh=mesh,
        in_specs=placed,
        out_specs=(P(("groups", "rows"), None, None, "cols"), P(("groups", "cols"))),
        check_vma=False,
    )
```

```python
import functools

import jax
import jax.numpy as jnp
from jax import lax
from jax.experimental import pallas as pl
from jax.experimental.pallas import tpu as pltpu
from jax.sharding import PartitionSpec as P

HIGHEST = lax.Precision.HIGHEST
PARAMS = pltpu.CompilerParams(vmem_limit_bytes=16 * 2**20)
VMEM = pl.BlockSpec(memory_space=pltpu.VMEM)
SMEM = pl.BlockSpec(memory_space=pltpu.SMEM)


def dot(left, right, dims=((1,), (0,))):
    return lax.dot_general(
        left, right, (dims, ((), ())), precision=HIGHEST, preferred_element_type=jnp.float32
    )


def lanes(values, index):
    return jnp.take_along_axis(
        values, jnp.broadcast_to(index, values.shape), axis=1, mode="promise_in_bounds"
    )


def code_kernel(pairing_ref, code_ref):
    meets, turns, n = pairing_ref.shape
    pairs = jnp.concatenate([pairing_ref[m] for m in range(meets)], axis=0)
    place = lax.broadcasted_iota(jnp.int32, pairs.shape, 1)
    told = lanes(pairs, place ^ 1) + jnp.where(place % 2 == 0, n, 0)
    pairs = pairs.astype(jnp.float32).T
    told = told.astype(jnp.float32).T
    col = lax.broadcasted_iota(jnp.int32, (n, n), 1).astype(jnp.float32)
    rows = []
    for index in range(meets * turns):
        here = pairs[:, index : index + 1] == col
        rows.append(jnp.sum(jnp.where(here, told[:, index : index + 1], 0.0), axis=0, keepdims=True))
    code_ref[...] = jnp.concatenate(rows, axis=0).astype(jnp.int32)


def quarter_squares(labels, conductivity_ref):
    labels = labels.T
    squares = jnp.zeros(labels.shape, jnp.float32)
    for region in range(conductivity_ref.shape[0]):
        squares = jnp.where(labels == region, conductivity_ref[region], squares)
    return 0.25 * squares


def local_kernel(conductivity_ref, own_ref, other_ref, labels_ref, gram_ref, turned_ref, applied_ref):
    ny, nz, width = own_ref.shape
    squares = quarter_squares(labels_ref[...], conductivity_ref)
    z = lax.broadcasted_iota(jnp.int32, (nz, ny), 0)
    above = jnp.where(z < nz - 1, pltpu.roll(squares, nz - 1, 0), 0.0)
    below = jnp.where(z > 0, pltpu.roll(squares, 1, 0), 0.0)
    inner = 1.0 + above + below
    above = jnp.where(z < nz - 2, above, 0.0)
    below = jnp.where(z > 1, below, 0.0)
    for y in range(ny):
        u = own_ref[y]
        scale = inner[:, y : y + 1]
        if y > 0:
            scale += squares[:, y - 1 : y]
        if y < ny - 1:
            scale += squares[:, y + 1 : y + 2]
        total = scale * u
        if y > 1:
            total -= squares[:, y - 1 : y] * own_ref[y - 2]
        if y < ny - 2:
            total -= squares[:, y + 1 : y + 2] * own_ref[y + 2]
        total -= above[:, y : y + 1] * pltpu.roll(u, nz - 2, 0)
        total -= below[:, y : y + 1] * pltpu.roll(u, 2, 0)
        applied_ref[y * nz : (y + 1) * nz, :] = total
    turned_ref[:width, :] = own_ref[...].reshape(ny * nz, width).T
    turned_ref[width:, :] = other_ref[...].reshape(ny * nz, width).T
    gram_ref[...] = dot(turned_ref[...], applied_ref[...])


def halo_kernel(
    place_ref, conductivity_ref, own_ref, halo_ref, after_ref, before_ref, gram_ref, turned_ref,
    kept_ref, sent_ref, applied_ref,
):
    ny, nz, width = own_ref.shape
    after = quarter_squares(after_ref[...], conductivity_ref)
    before = quarter_squares(before_ref[...], conductivity_ref)
    after = jnp.where(place_ref[1] < place_ref[2] - 1, after, 0.0)
    before = jnp.where(place_ref[1] > 0, before, 0.0)
    for y in range(ny):
        ahead = after[:, y : y + 1]
        applied_ref[y * nz : (y + 1) * nz, :] = (ahead + before[:, y : y + 1]) * own_ref[y] - (
            2.0 * ahead
        ) * halo_ref[y]
    gram = gram_ref[...] + dot(turned_ref[...], applied_ref[...])
    half = width // 2
    first = place_ref[0] == 0
    own = gram[:width]
    cross = gram[width:]
    cross = 0.5 * jnp.where(first, cross.T, cross)
    kept_ref[:width, :] = 0.5 * (own + own.T)
    kept_ref[width:, :] = jnp.where(first, cross[:half], cross[half:])
    sent_ref[...] = jnp.where(first, cross[half:], cross[:half])


def rotation(diagonal, opposite, coupling, first):
    g_first = jnp.where(first, diagonal, opposite)
    g_second = jnp.where(first, opposite, diagonal)
    spread = g_first - g_second
    radius = jnp.sqrt(spread * spread + 4.0 * coupling * coupling)
    sign = jnp.where(spread > 0, 1.0, jnp.where(spread < 0, -1.0, 0.0))
    tangent = (
        -2.0 * coupling * sign / (jnp.abs(spread) + radius + 1e-06 * (g_first + g_second + 1.0))
    )
    cosine = 1.0 / jnp.sqrt(1.0 + tangent * tangent)
    sine = cosine * tangent
    return cosine[:1], jnp.where(first, -sine, sine)[:1]


def tournament_kernel(
    meets, turns, place_ref, mine_ref, theirs_ref, code_ref, own_ref, other_ref, rotated_ref, sigma_ref
):
    n = own_ref.shape[2]
    h = n // 2
    side = place_ref[0] == 0
    mine, theirs = mine_ref[...], theirs_ref[...]
    zero_side = jnp.where(side, mine, theirs)
    one_side = jnp.where(side, theirs, mine)
    cross = jnp.concatenate([zero_side[n:], one_side[n:]], axis=0)
    row = lax.broadcasted_iota(jnp.int32, (n, n), 0)
    col = lax.broadcasted_iota(jnp.int32, (n, n), 1)
    eye = row == col
    identity = jnp.where(eye, 1.0, 0.0)
    blank = jnp.zeros((n, h), jnp.float32)
    gram = jnp.concatenate(
        [
            jnp.concatenate([zero_side[:n], cross], axis=1),
            jnp.concatenate([cross.T, one_side[:n]], axis=1),
        ],
        axis=0,
    )
    total = None
    upper, lower = [0, 2], [1, 3]
    for meeting in range(meets):
        met = [gram[:n, :n], gram[n:, n:]]
        factor = [identity, identity]
        for turn in range(turns):
            index = meeting * turns + turn
            told = code_ref[index : index + 1, :]
            partner = told % n
            first = told >= n
            paired = row == partner
            for d in range(2):
                held = met[d]
                diagonal = jnp.sum(jnp.where(eye, held, 0.0), axis=0, keepdims=True)
                coupling = jnp.sum(jnp.where(paired, held, 0.0), axis=0, keepdims=True)
                diagonal = jnp.broadcast_to(diagonal, (8, n))
                coupling = jnp.broadcast_to(coupling, (8, n))
                cosine, sine = rotation(diagonal, lanes(diagonal, partner), coupling, first)
                held = (held * cosine + lanes(held, partner) * sine).T
                met[d] = held * cosine + lanes(held, partner) * sine
                factor[d] = factor[d] * cosine + lanes(factor[d], partner) * sine
        blocks = {}
        for d in range(2):
            for block, part in ((upper[d], factor[d][:, :h]), (lower[d], factor[d][:, h:])):
                blocks[block] = jnp.concatenate([part, blank] if d == 0 else [blank, part], axis=0)
        if meeting == meets - 1:
            after = range(4)
            norms = {}
            for d in range(2):
                norm = jnp.sqrt(jnp.sum(jnp.where(eye, met[d], 0.0), axis=0, keepdims=True))
                norms[upper[d]], norms[lower[d]] = norm[:, :h], norm[:, h:]
        else:
            upper, lower = [upper[0], lower[0]], [lower[1], upper[1]]
            after = [upper[0], lower[0], upper[1], lower[1]]
        wide = jnp.concatenate([blocks[block] for block in after], axis=1)
        total = wide if total is None else dot(total, wide)
        if meeting < meets - 1:
            gram = dot(wide, dot(gram, wide), ((0,), (0,)))
    picked = jnp.where(side, total[:, :n], total[:, n:])
    near = jnp.where(side, picked[:n], picked[n:])
    far = jnp.where(side, picked[n:], picked[:n])
    flat = (-1, n)
    rotated = dot(own_ref[...].reshape(flat), near) + dot(other_ref[...].reshape(flat), far)
    rotated_ref[...] = rotated.reshape(rotated_ref.shape)
    sigma_ref[...] = jnp.where(
        side,
        jnp.concatenate([norms[0], norms[1]], axis=1),
        jnp.concatenate([norms[2], norms[3]], axis=1),
    )


def shards(snapshots, labels, conductivity, pairing):
    planes, ny, nz, width = snapshots.shape
    cells = planes * ny * nz
    half = width // 2
    count = lax.axis_size("rows")
    swap = [(0, 1), (1, 0)]
    own = snapshots[0]
    labels = labels[0]
    halo = lax.ppermute(own, "rows", [(i + 2, i) for i in range(count - 2)])
    other = lax.ppermute(own, "cols", swap)
    after = lax.ppermute(labels, "rows", [(i + 1, i) for i in range(count - 1)])
    before = lax.ppermute(labels, "rows", [(i, i + 1) for i in range(count - 1)])
    place = jnp.stack(
        [lax.axis_index("cols"), lax.axis_index("rows"), jnp.asarray(count, jnp.int32)]
    ).astype(jnp.int32)

    code = pl.pallas_call(
        code_kernel,
        out_shape=jax.ShapeDtypeStruct((pairing.shape[0] * pairing.shape[1], width), jnp.int32),
        in_specs=[VMEM],
        out_specs=VMEM,
        compiler_params=PARAMS,
    )(pairing)
    gram, turned = pl.pallas_call(
        local_kernel,
        out_shape=(
            jax.ShapeDtypeStruct((2 * width, width), jnp.float32),
            jax.ShapeDtypeStruct((2 * width, cells), jnp.float32),
        ),
        in_specs=[SMEM] + [VMEM] * 3,
        out_specs=[VMEM] * 2,
        scratch_shapes=[pltpu.VMEM((cells, width), jnp.float32)],
        compiler_params=PARAMS,
    )(conductivity, own, other, labels)
    kept, sent = pl.pallas_call(
        halo_kernel,
        out_shape=(
            jax.ShapeDtypeStruct((width + half, width), jnp.float32),
            jax.ShapeDtypeStruct((half, width), jnp.float32),
        ),
        in_specs=[SMEM] * 2 + [VMEM] * 6,
        out_specs=[VMEM] * 2,
        scratch_shapes=[pltpu.VMEM((cells, width), jnp.float32)],
        compiler_params=PARAMS,
    )(place, conductivity, own, halo, after, before, gram, turned)
    received = lax.ppermute(sent, "cols", swap)
    share = jnp.concatenate([kept[:width], kept[width:] + received], axis=0)
    apart = 1
    while apart < count:
        share = share + lax.ppermute(share, "rows", [(i, i ^ apart) for i in range(count)])
        apart *= 2
    theirs = lax.ppermute(share, "cols", swap)
    rotated, sigma = pl.pallas_call(
        functools.partial(tournament_kernel, pairing.shape[0], pairing.shape[1]),
        out_shape=(
            jax.ShapeDtypeStruct((ny, nz, width), jnp.float32),
            jax.ShapeDtypeStruct((1, width), jnp.float32),
        ),
        in_specs=[SMEM] + [VMEM] * 5,
        out_specs=[VMEM] * 2,
        compiler_params=PARAMS,
    )(place, share, theirs, code, own, other)
    return rotated.reshape(snapshots.shape), sigma.reshape(width)


def solution(mesh):
    placed = (
        P(("groups", "rows"), None, None, "cols"),
        P(("groups", "rows"), None, None),
        P("groups"),
        P(),
    )
    return jax.shard_map(
        shards,
        mesh=mesh,
        in_specs=placed,
        out_specs=(P(("groups", "rows"), None, None, "cols"), P(("groups", "cols"))),
        check_vma=False,
    )
```

```python
import functools

import jax
import jax.numpy as jnp
from jax import lax
from jax.experimental import pallas as pl
from jax.experimental.pallas import tpu as pltpu
from jax.sharding import PartitionSpec as P

HIGHEST = lax.Precision.HIGHEST
PARAMS = pltpu.CompilerParams(vmem_limit_bytes=16 * 2**20)
VMEM = pl.BlockSpec(memory_space=pltpu.VMEM)
SMEM = pl.BlockSpec(memory_space=pltpu.SMEM)


def dot(left, right, dims=((1,), (0,))):
    return lax.dot_general(
        left, right, (dims, ((), ())), precision=HIGHEST, preferred_element_type=jnp.float32
    )


def lanes(values, index):
    return jnp.take_along_axis(
        values, jnp.broadcast_to(index, values.shape), axis=1, mode="promise_in_bounds"
    )


def code_kernel(pairing_ref, code_ref):
    meets, turns, n = pairing_ref.shape
    pairs = jnp.concatenate([pairing_ref[m] for m in range(meets)], axis=0)
    place = lax.broadcasted_iota(jnp.int32, pairs.shape, 1)
    told = lanes(pairs, place ^ 1) + jnp.where(place % 2 == 0, n, 0)
    pairs = pairs.astype(jnp.float32).T
    told = told.astype(jnp.float32).T
    col = lax.broadcasted_iota(jnp.int32, (n, n), 1).astype(jnp.float32)
    rows = []
    for index in range(meets * turns):
        here = pairs[:, index : index + 1] == col
        rows.append(jnp.sum(jnp.where(here, told[:, index : index + 1], 0.0), axis=0, keepdims=True))
    code_ref[...] = jnp.concatenate(rows, axis=0).astype(jnp.int32)


def quarter_squares(labels, conductivity_ref):
    labels = labels.T
    squares = jnp.zeros(labels.shape, jnp.float32)
    for region in range(conductivity_ref.shape[0]):
        squares = jnp.where(labels == region, conductivity_ref[region], squares)
    return 0.25 * squares


def local_kernel(conductivity_ref, own_ref, other_ref, labels_ref, gram_ref, turned_ref, applied_ref):
    ny, nz, width = own_ref.shape
    squares = quarter_squares(labels_ref[...], conductivity_ref)
    z = lax.broadcasted_iota(jnp.int32, (nz, ny), 0)
    above = jnp.where(z < nz - 1, pltpu.roll(squares, nz - 1, 0), 0.0)
    below = jnp.where(z > 0, pltpu.roll(squares, 1, 0), 0.0)
    inner = 1.0 + above + below
    above = jnp.where(z < nz - 2, above, 0.0)
    below = jnp.where(z > 1, below, 0.0)
    for y in range(ny):
        u = own_ref[y]
        scale = inner[:, y : y + 1]
        if y > 0:
            scale += squares[:, y - 1 : y]
        if y < ny - 1:
            scale += squares[:, y + 1 : y + 2]
        total = scale * u
        if y > 1:
            total -= squares[:, y - 1 : y] * own_ref[y - 2]
        if y < ny - 2:
            total -= squares[:, y + 1 : y + 2] * own_ref[y + 2]
        total -= above[:, y : y + 1] * pltpu.roll(u, nz - 2, 0)
        total -= below[:, y : y + 1] * pltpu.roll(u, 2, 0)
        applied_ref[y * nz : (y + 1) * nz, :] = total
    turned_ref[:width, :] = own_ref[...].reshape(ny * nz, width).T
    turned_ref[width:, :] = other_ref[...].reshape(ny * nz, width).T
    gram_ref[...] = dot(turned_ref[...], applied_ref[...])


def halo_kernel(
    place_ref, conductivity_ref, own_ref, halo_ref, after_ref, before_ref, gram_ref, turned_ref,
    kept_ref, sent_ref, applied_ref,
):
    ny, nz, width = own_ref.shape
    after = quarter_squares(after_ref[...], conductivity_ref)
    before = quarter_squares(before_ref[...], conductivity_ref)
    after = jnp.where(place_ref[1] < place_ref[2] - 1, after, 0.0)
    before = jnp.where(place_ref[1] > 0, before, 0.0)
    for y in range(ny):
        ahead = after[:, y : y + 1]
        applied_ref[y * nz : (y + 1) * nz, :] = (ahead + before[:, y : y + 1]) * own_ref[y] - (
            2.0 * ahead
        ) * halo_ref[y]
    gram = gram_ref[...] + dot(turned_ref[...], applied_ref[...])
    half = width // 2
    first = place_ref[0] == 0
    own = gram[:width]
    cross = gram[width:]
    cross = 0.5 * jnp.where(first, cross.T, cross)
    kept_ref[:width, :] = 0.5 * (own + own.T)
    kept_ref[width:, :] = jnp.where(first, cross[:half], cross[half:])
    sent_ref[...] = jnp.where(first, cross[half:], cross[:half])


def split(values, count):
    parts = []
    for index in range(count):
        part = values.astype(jnp.bfloat16)
        parts.append(part)
        if index < count - 1:
            values = values - part.astype(jnp.float32)
    return parts


TWO = ((0, 0), (0, 1), (1, 0))
THREE = TWO + ((0, 2), (1, 1), (2, 0))


def long_dot(left, right, terms):
    count = 1 + max(i for i, _ in terms)
    left, right = split(left, count), split(right, count)
    return jnp.dot(
        jnp.concatenate([left[i] for i, _ in terms], axis=1),
        jnp.concatenate([right[j] for _, j in terms], axis=0),
        preferred_element_type=jnp.float32,
    )


def column_sums(values):
    return jnp.broadcast_to(jnp.sum(values, axis=0, keepdims=True), (8, values.shape[1]))


def rotation(diagonal, opposite, coupling, first):
    g_first = jnp.where(first, diagonal, opposite)
    g_second = jnp.where(first, opposite, diagonal)
    spread = g_first - g_second
    radius = jnp.sqrt(spread * spread + 4.0 * coupling * coupling)
    turned = jnp.where(spread > 0, -2.0, jnp.where(spread < 0, 2.0, 0.0)) * coupling
    tangent = turned * pl.reciprocal(
        jnp.abs(spread) + radius + 1e-06 * (g_first + g_second + 1.0), approx=False
    )
    cosine = lax.rsqrt(1.0 + tangent * tangent)
    sine = cosine * tangent
    return cosine, jnp.where(first, -sine, sine)


def tournament_kernel(
    meets, turns, place_ref, mine_ref, theirs_ref, code_ref, own_ref, other_ref, rotated_ref, sigma_ref
):
    n = own_ref.shape[2]
    h = n // 2
    side = place_ref[0] == 0
    mine, theirs = mine_ref[...], theirs_ref[...]
    zero_side = jnp.where(side, mine, theirs)
    one_side = jnp.where(side, theirs, mine)
    eye = lax.broadcasted_iota(jnp.int32, (n, n), 0) == lax.broadcasted_iota(jnp.int32, (n, n), 1)
    row = lax.broadcasted_iota(jnp.int32, (n, n), 0)
    blank = jnp.zeros((n, n), jnp.float32)
    low_half = lax.broadcasted_iota(jnp.int32, (h, n), 1) < h
    low = lax.broadcasted_iota(jnp.int32, (2 * n, n), 1) < h

    cross01 = jnp.concatenate([zero_side[n:], one_side[n:]], axis=0)
    near = [zero_side[:n], one_side[:n]]
    cross = [cross01.T, cross01]
    total = None
    slots = [[0, 1], [2, 3]]
    upper, lower = [0, 2], [1, 3]
    for meeting in range(meets):
        last = meeting == meets - 1
        uppers = {frozenset((upper[d], lower[d])): upper[d] for d in range(2)}
        swapped = [uppers[frozenset(slots[d])] != slots[d][0] for d in range(2)]
        factor = [None, None]
        diagonal = [column_sums(jnp.where(eye, near[d], 0.0)) for d in range(2)]
        for turn in range(turns):
            index = meeting * turns + turn
            told = code_ref[index : index + 1, :]
            other_way = pltpu.roll(jnp.broadcast_to(told, (8, n)), h, 1)[:1]
            for d in range(2):
                partner = (other_way % n) ^ h if swapped[d] else told % n
                first = (other_way if swapped[d] else told) >= n
                if turn == 0:
                    paired = row == partner
                    coupling = column_sums(jnp.where(paired, near[d], 0.0))
                else:
                    opposite = lanes(factor[d], partner)
                    coupling = column_sums(opposite * near[d])
                across = lanes(diagonal[d], partner)
                cosine, sine = rotation(diagonal[d], across, coupling, first)
                diagonal[d] = (
                    cosine * cosine * diagonal[d] + 2.0 * cosine * sine * coupling + sine * sine * across
                )
                cosine, sine = cosine[:1], sine[:1]
                if turn == 0:
                    factor[d] = jnp.where(eye, cosine, jnp.where(paired, sine, 0.0))
                else:
                    factor[d] = factor[d] * cosine + opposite * sine
                if not last or turn < turns - 1:
                    near[d] = near[d] * cosine + lanes(near[d], partner) * sine
                if not last:
                    cross[d] = cross[d] * cosine + lanes(cross[d], partner) * sine
        if last:
            break
        if total is None:
            total = [
                jnp.concatenate([factor[0], blank], axis=0),
                jnp.concatenate([blank, factor[1]], axis=0),
            ]
        else:
            total = [long_dot(total[d], factor[d], TWO) for d in range(2)]
        top = long_dot(factor[0].T, jnp.concatenate([near[0], cross[1]], axis=1), THREE)
        bottom = long_dot(factor[1].T, jnp.concatenate([cross[0], near[1]], axis=1), THREE)
        g00, g01, g10, g11 = top[:, :n], top[:, n:], bottom[:, :n], bottom[:, n:]
        upper, lower = [upper[0], lower[0]], [lower[1], upper[1]]
        meets_next = [frozenset((upper[d], lower[d])) for d in range(2)]
        if frozenset((slots[0][0], slots[1][1])) not in meets_next:
            slots[1] = slots[1][::-1]
            g01, g11 = pltpu.roll(g01, h, 1), pltpu.roll(g11, h, 1)
            g10 = jnp.concatenate([g10[h:], g10[:h]], axis=0)
            g11 = jnp.concatenate([g11[h:], g11[:h]], axis=0)
            total[1] = pltpu.roll(total[1], h, 1)
        slots = [[slots[0][0], slots[1][1]], [slots[1][0], slots[0][1]]]

        def mixed(first, second, third, fourth):
            return jnp.concatenate(
                [
                    jnp.where(low_half, first[:h], second[:h]),
                    jnp.where(low_half, third[h:], fourth[h:]),
                ],
                axis=0,
            )

        near = [mixed(g00, g01, g10, g11), mixed(g11, g10, g01, g00)]
        cross = [mixed(g10, g11, g00, g01), mixed(g01, g00, g11, g10)]
        total = [jnp.where(low, total[0], total[1]), jnp.where(low, total[1], total[0])]

    flat = jnp.concatenate(
        [own_ref[...].reshape(-1, n), other_ref[...].reshape(-1, n)], axis=1
    )
    both = jnp.concatenate(total, axis=1)
    both = jnp.concatenate(
        [jnp.where(side, both[:n], both[n:]), jnp.where(side, both[n:], both[:n])], axis=0
    )
    before_last = long_dot(flat, both, TWO)
    gap = jnp.zeros((n, h), jnp.float32)
    blocks, norms = {}, {}
    for d in range(2):
        norm = jnp.sqrt(diagonal[d][:1])
        for i in range(2):
            part = factor[d][:, i * h : (i + 1) * h]
            blocks[slots[d][i]] = jnp.concatenate([part, gap] if d == 0 else [gap, part], axis=0)
            norms[slots[d][i]] = norm[:, i * h : (i + 1) * h]
    picked = jnp.where(
        side,
        jnp.concatenate([blocks[0], blocks[1]], axis=1),
        jnp.concatenate([blocks[2], blocks[3]], axis=1),
    )
    rotated_ref[...] = long_dot(before_last, picked, TWO).reshape(rotated_ref.shape)
    sigma_ref[...] = jnp.where(
        side,
        jnp.concatenate([norms[0], norms[1]], axis=1),
        jnp.concatenate([norms[2], norms[3]], axis=1),
    )


def shards(snapshots, labels, conductivity, pairing):
    planes, ny, nz, width = snapshots.shape
    cells = planes * ny * nz
    half = width // 2
    count = lax.axis_size("rows")
    swap = [(0, 1), (1, 0)]
    own = snapshots[0]
    labels = labels[0]
    halo = lax.ppermute(own, "rows", [(i + 2, i) for i in range(count - 2)])
    other = lax.ppermute(own, "cols", swap)
    after = lax.ppermute(labels, "rows", [(i + 1, i) for i in range(count - 1)])
    before = lax.ppermute(labels, "rows", [(i, i + 1) for i in range(count - 1)])
    place = jnp.stack(
        [lax.axis_index("cols"), lax.axis_index("rows"), jnp.asarray(count, jnp.int32)]
    ).astype(jnp.int32)

    code = pl.pallas_call(
        code_kernel,
        out_shape=jax.ShapeDtypeStruct((pairing.shape[0] * pairing.shape[1], width), jnp.int32),
        in_specs=[VMEM],
        out_specs=VMEM,
        compiler_params=PARAMS,
    )(pairing)
    gram, turned = pl.pallas_call(
        local_kernel,
        out_shape=(
            jax.ShapeDtypeStruct((2 * width, width), jnp.float32),
            jax.ShapeDtypeStruct((2 * width, cells), jnp.float32),
        ),
        in_specs=[SMEM] + [VMEM] * 3,
        out_specs=[VMEM] * 2,
        scratch_shapes=[pltpu.VMEM((cells, width), jnp.float32)],
        compiler_params=PARAMS,
    )(conductivity, own, other, labels)
    kept, sent = pl.pallas_call(
        halo_kernel,
        out_shape=(
            jax.ShapeDtypeStruct((width + half, width), jnp.float32),
            jax.ShapeDtypeStruct((half, width), jnp.float32),
        ),
        in_specs=[SMEM] * 2 + [VMEM] * 6,
        out_specs=[VMEM] * 2,
        scratch_shapes=[pltpu.VMEM((cells, width), jnp.float32)],
        compiler_params=PARAMS,
    )(place, conductivity, own, halo, after, before, gram, turned)
    received = lax.ppermute(sent, "cols", swap)
    share = jnp.concatenate([kept[:width], kept[width:] + received], axis=0)
    apart = 1
    while apart < count:
        share = share + lax.ppermute(share, "rows", [(i, i ^ apart) for i in range(count)])
        apart *= 2
    theirs = lax.ppermute(share, "cols", swap)
    rotated, sigma = pl.pallas_call(
        functools.partial(tournament_kernel, pairing.shape[0], pairing.shape[1]),
        out_shape=(
            jax.ShapeDtypeStruct((ny, nz, width), jnp.float32),
            jax.ShapeDtypeStruct((1, width), jnp.float32),
        ),
        in_specs=[SMEM] + [VMEM] * 5,
        out_specs=[VMEM] * 2,
        compiler_params=PARAMS,
    )(place, share, theirs, code, own, other)
    return rotated.reshape(snapshots.shape), sigma.reshape(width)


def solution(mesh):
    placed = (
        P(("groups", "rows"), None, None, "cols"),
        P(("groups", "rows"), None, None),
        P("groups"),
        P(),
    )
    return jax.shard_map(
        shards,
        mesh=mesh,
        in_specs=placed,
        out_specs=(P(("groups", "rows"), None, None, "cols"), P(("groups", "cols"))),
        check_vma=False,
    )
```

```python
import functools

import jax
import jax.numpy as jnp
from jax import lax
from jax.experimental import pallas as pl
from jax.experimental.pallas import tpu as pltpu
from jax.sharding import PartitionSpec as P

PARAMS = pltpu.CompilerParams(vmem_limit_bytes=16 * 2**20)
HBM = pl.BlockSpec(memory_space=pltpu.HBM)
VMEM = pl.BlockSpec(memory_space=pltpu.VMEM)
SMEM = pl.BlockSpec(memory_space=pltpu.SMEM)


def lanes(values, index):
    return jnp.take_along_axis(
        values, jnp.broadcast_to(index, values.shape), axis=1, mode="promise_in_bounds"
    )


def code_kernel(pairing_ref, code_ref):
    meets, turns, n = pairing_ref.shape
    pairs = jnp.concatenate([pairing_ref[m] for m in range(meets)], axis=0)
    place = lax.broadcasted_iota(jnp.int32, pairs.shape, 1)
    told = lanes(pairs, place ^ 1) + jnp.where(place % 2 == 0, n, 0)
    pairs = pairs.astype(jnp.float32).T
    told = told.astype(jnp.float32).T
    col = lax.broadcasted_iota(jnp.int32, (n, n), 1).astype(jnp.float32)
    rows = []
    for index in range(meets * turns):
        here = pairs[:, index : index + 1] == col
        rows.append(jnp.sum(jnp.where(here, told[:, index : index + 1], 0.0), axis=0, keepdims=True))
    code_ref[...] = jnp.concatenate(rows, axis=0).astype(jnp.int32)


def split(values, count):
    parts = []
    for index in range(count):
        part = values.astype(jnp.bfloat16)
        parts.append(part)
        if index < count - 1:
            values = values - part.astype(jnp.float32)
    return parts


TWO = ((0, 0), (0, 1), (1, 0))
THREE = TWO + ((0, 2), (1, 1), (2, 0))


def long_dot(left, right, terms):
    count = 1 + max(i for i, _ in terms)
    left, right = split(left, count), split(right, count)
    return jnp.dot(
        laid(left, terms, 0, 1), laid(right, terms, 1, 0), preferred_element_type=jnp.float32
    )


def laid(parts, terms, side, axis):
    return jnp.concatenate([parts[term[side]] for term in terms], axis=axis)


def column_sums(values):
    return jnp.broadcast_to(jnp.sum(values, axis=0, keepdims=True), (8, values.shape[1]))


def quarter_squares(labels, table):
    squares = jnp.zeros(labels.shape, jnp.float32)
    for region in range(table.shape[0]):
        squares = jnp.where(labels == region, table[region : region + 1, : labels.shape[1]], squares)
    return squares


def local_kernel(
    conductivity_ref, own_hbm_ref, labels_hbm_ref, other_ref,
    gram_ref, turned_ref, own_ref, table_ref,
    applied_ref, labels_ref, regions_ref, sems,
):
    ny, nz, width = own_ref.shape
    cells = ny * nz
    fetches = [
        pltpu.make_async_copy(source, target, sems.at[index])
        for index, (source, target) in enumerate(
            ((own_hbm_ref, own_ref), (labels_hbm_ref, labels_ref), (conductivity_ref, regions_ref))
        )
    ]
    for fetch in fetches:
        fetch.start()
    turned_ref[width:, :] = laid(split(other_ref[...].reshape(cells, width).T, 3), THREE, 0, 1)
    for fetch in fetches:
        fetch.wait()
    table_ref[...] = jnp.concatenate(
        [jnp.full((1, width), 0.25 * regions_ref[region]) for region in range(table_ref.shape[0])],
        axis=0,
    )
    squares = quarter_squares(labels_ref[...], table_ref[...])
    z = lax.broadcasted_iota(jnp.int32, (nz, ny), 0)
    above = jnp.where(z < nz - 1, pltpu.roll(squares, nz - 1, 0), 0.0)
    below = jnp.where(z > 0, pltpu.roll(squares, 1, 0), 0.0)
    inner = 1.0 + above + below
    above = jnp.where(z < nz - 2, above, 0.0)
    below = jnp.where(z > 1, below, 0.0)
    for y in range(ny):
        u = own_ref[y]
        scale = inner[:, y : y + 1]
        if y > 0:
            scale += squares[:, y - 1 : y]
        if y < ny - 1:
            scale += squares[:, y + 1 : y + 2]
        total = scale * u
        if y > 1:
            total -= squares[:, y - 1 : y] * own_ref[y - 2]
        if y < ny - 2:
            total -= squares[:, y + 1 : y + 2] * own_ref[y + 2]
        total -= above[:, y : y + 1] * pltpu.roll(u, nz - 2, 0)
        total -= below[:, y : y + 1] * pltpu.roll(u, 2, 0)
        applied_ref[y * nz : (y + 1) * nz, :] = total
    turned_ref[:width, :] = laid(split(own_ref[...].reshape(cells, width).T, 3), THREE, 0, 1)
    gram_ref[...] = jnp.dot(
        turned_ref[...],
        laid(split(applied_ref[...], 3), THREE, 1, 0),
        preferred_element_type=jnp.float32,
    )


def halo_kernel(
    place_ref, table_ref, own_ref, halo_ref, mine_ref, theirs_ref, gram_ref, turned_ref,
    kept_ref, sent_ref, applied_ref,
):
    ny, nz, width = own_ref.shape
    mine = quarter_squares(mine_ref[...], table_ref[...])
    theirs = quarter_squares(theirs_ref[...], table_ref[...])
    after = jnp.where(place_ref[0] == 0, mine, theirs)
    before = jnp.where(place_ref[0] == 0, theirs, mine)
    after = jnp.where(place_ref[1] < place_ref[2] - 1, after, 0.0)
    before = jnp.where(place_ref[1] > 0, before, 0.0)
    for y in range(ny):
        ahead = after[:, y : y + 1]
        applied_ref[y * nz : (y + 1) * nz, :] = (ahead + before[:, y : y + 1]) * own_ref[y] - (
            2.0 * ahead
        ) * halo_ref[y]
    gram = gram_ref[...] + jnp.dot(
        turned_ref[...],
        laid(split(applied_ref[...], 3), THREE, 1, 0),
        preferred_element_type=jnp.float32,
    )
    half = width // 2
    first = place_ref[0] == 0
    own = gram[:width]
    cross = gram[width:]
    cross = 0.5 * jnp.where(first, cross.T, cross)
    own = 0.5 * (own + own.T)
    row = lax.broadcasted_iota(jnp.int32, (half, width), 0)
    col = lax.broadcasted_iota(jnp.int32, (half, width), 1)
    kept_ref[:half, :] = jnp.where(
        (col >= row), own[:half], pltpu.roll(own[half:], half, 1)
    )
    kept_ref[half : half + 8, :] = column_sums(
        jnp.where(
            lax.broadcasted_iota(jnp.int32, (width, width), 0)
            == lax.broadcasted_iota(jnp.int32, (width, width), 1),
            own,
            0.0,
        )
    )
    kept_ref[half + 8 :, :] = jnp.where(first, cross[:half], cross[half:])
    sent_ref[...] = jnp.where(first, cross[half:], cross[:half])


def unpacked(share):
    n = share.shape[1]
    h = n // 2
    top = share[:h]
    row = lax.broadcasted_iota(jnp.int32, (h, n), 0)
    col = lax.broadcasted_iota(jnp.int32, (h, n), 1)
    mirror = top.T
    wide = jnp.concatenate([mirror[:h], mirror[:h]], axis=1)
    first = jnp.where(col >= row, top, wide)
    second = jnp.where(col - h < row, pltpu.roll(top, h, 1), wide)
    second = jnp.where(col - h == row, share[h : h + 1], second)
    tall = jnp.concatenate([mirror[h:], mirror[h:]], axis=1)
    return jnp.concatenate([first, jnp.where(col < h, tall, second)], axis=0)


def rotation(diagonal, opposite, coupling, first):
    g_first = jnp.where(first, diagonal, opposite)
    g_second = jnp.where(first, opposite, diagonal)
    spread = g_first - g_second
    radius = jnp.sqrt(spread * spread + 4.0 * coupling * coupling)
    turned = jnp.where(spread > 0, -2.0, jnp.where(spread < 0, 2.0, 0.0)) * coupling
    tangent = turned * pl.reciprocal(
        jnp.abs(spread) + radius + 1e-06 * (g_first + g_second + 1.0), approx=False
    )
    cosine = lax.rsqrt(1.0 + tangent * tangent)
    sine = cosine * tangent
    return cosine, jnp.where(first, -sine, sine)


def tournament_kernel(
    meets, turns, place_ref, mine_ref, theirs_ref, code_ref, own_ref, other_ref, rotated_ref, sigma_ref
):
    n = own_ref.shape[2]
    h = n // 2
    side = place_ref[0] == 0
    mine, theirs = mine_ref[...], theirs_ref[...]
    zero_side = jnp.where(side, mine, theirs)
    one_side = jnp.where(side, theirs, mine)
    eye = lax.broadcasted_iota(jnp.int32, (n, n), 0) == lax.broadcasted_iota(jnp.int32, (n, n), 1)
    row = lax.broadcasted_iota(jnp.int32, (n, n), 0)
    blank = jnp.zeros((n, n), jnp.float32)
    low_half = lax.broadcasted_iota(jnp.int32, (h, n), 1) < h
    low = lax.broadcasted_iota(jnp.int32, (2 * n, n), 1) < h

    cross01 = jnp.concatenate([zero_side[h + 8 :], one_side[h + 8 :]], axis=0)
    near = [unpacked(zero_side), unpacked(one_side)]
    cross = [cross01.T, cross01]
    total = None
    slots = [[0, 1], [2, 3]]
    upper, lower = [0, 2], [1, 3]
    for meeting in range(meets):
        last = meeting == meets - 1
        uppers = {frozenset((upper[d], lower[d])): upper[d] for d in range(2)}
        swapped = [uppers[frozenset(slots[d])] != slots[d][0] for d in range(2)]
        factor = [None, None]
        diagonal = [column_sums(jnp.where(eye, near[d], 0.0)) for d in range(2)]
        for turn in range(turns):
            index = meeting * turns + turn
            told = code_ref[index : index + 1, :]
            other_way = pltpu.roll(jnp.broadcast_to(told, (8, n)), h, 1)[:1]
            for d in range(2):
                partner = (other_way % n) ^ h if swapped[d] else told % n
                first = (other_way if swapped[d] else told) >= n
                if turn == 0:
                    paired = row == partner
                    coupling = column_sums(jnp.where(paired, near[d], 0.0))
                else:
                    opposite = lanes(factor[d], partner)
                    coupling = column_sums(opposite * near[d])
                across = lanes(diagonal[d], partner)
                cosine, sine = rotation(diagonal[d], across, coupling, first)
                diagonal[d] = (
                    cosine * cosine * diagonal[d] + 2.0 * cosine * sine * coupling + sine * sine * across
                )
                cosine, sine = cosine[:1], sine[:1]
                if turn == 0:
                    factor[d] = jnp.where(eye, cosine, jnp.where(paired, sine, 0.0))
                else:
                    factor[d] = factor[d] * cosine + opposite * sine
                if not last or turn < turns - 1:
                    near[d] = near[d] * cosine + lanes(near[d], partner) * sine
                if not last:
                    cross[d] = cross[d] * cosine + lanes(cross[d], partner) * sine
        if last:
            break
        if total is None:
            total = [
                jnp.concatenate([factor[0], blank], axis=0),
                jnp.concatenate([blank, factor[1]], axis=0),
            ]
        else:
            total = [long_dot(total[d], factor[d], TWO) for d in range(2)]
        top = long_dot(factor[0].T, jnp.concatenate([near[0], cross[1]], axis=1), THREE)
        bottom = long_dot(factor[1].T, jnp.concatenate([cross[0], near[1]], axis=1), THREE)
        g00, g01, g10, g11 = top[:, :n], top[:, n:], bottom[:, :n], bottom[:, n:]
        upper, lower = [upper[0], lower[0]], [lower[1], upper[1]]
        meets_next = [frozenset((upper[d], lower[d])) for d in range(2)]
        if frozenset((slots[0][0], slots[1][1])) not in meets_next:
            slots[1] = slots[1][::-1]
            g01, g11 = pltpu.roll(g01, h, 1), pltpu.roll(g11, h, 1)
            g10 = jnp.concatenate([g10[h:], g10[:h]], axis=0)
            g11 = jnp.concatenate([g11[h:], g11[:h]], axis=0)
            total[1] = pltpu.roll(total[1], h, 1)
        slots = [[slots[0][0], slots[1][1]], [slots[1][0], slots[0][1]]]

        def mixed(first, second, third, fourth):
            return jnp.concatenate(
                [
                    jnp.where(low_half, first[:h], second[:h]),
                    jnp.where(low_half, third[h:], fourth[h:]),
                ],
                axis=0,
            )

        near = [mixed(g00, g01, g10, g11), mixed(g11, g10, g01, g00)]
        cross = [mixed(g10, g11, g00, g01), mixed(g01, g00, g11, g10)]
        total = [jnp.where(low, total[0], total[1]), jnp.where(low, total[1], total[0])]

    flat = jnp.concatenate(
        [own_ref[...].reshape(-1, n), other_ref[...].reshape(-1, n)], axis=1
    )
    both = jnp.concatenate(total, axis=1)
    both = jnp.concatenate(
        [jnp.where(side, both[:n], both[n:]), jnp.where(side, both[n:], both[:n])], axis=0
    )
    before_last = long_dot(flat, both, TWO)
    gap = jnp.zeros((n, h), jnp.float32)
    blocks, norms = {}, {}
    for d in range(2):
        norm = jnp.sqrt(diagonal[d][:1])
        for i in range(2):
            part = factor[d][:, i * h : (i + 1) * h]
            blocks[slots[d][i]] = jnp.concatenate([part, gap] if d == 0 else [gap, part], axis=0)
            norms[slots[d][i]] = norm[:, i * h : (i + 1) * h]
    picked = jnp.where(
        side,
        jnp.concatenate([blocks[0], blocks[1]], axis=1),
        jnp.concatenate([blocks[2], blocks[3]], axis=1),
    )
    rotated_ref[...] = long_dot(before_last, picked, TWO).reshape(rotated_ref.shape)
    sigma_ref[...] = jnp.where(
        side,
        jnp.concatenate([norms[0], norms[1]], axis=1),
        jnp.concatenate([norms[2], norms[3]], axis=1),
    )


def shards(snapshots, labels, conductivity, pairing):
    planes, ny, nz, width = snapshots.shape
    cells = planes * ny * nz
    half = width // 2
    count = lax.axis_size("rows")
    swap = [(0, 1), (1, 0)]
    own = snapshots[0]
    labels = labels[0].T
    halo = lax.ppermute(own, "rows", [(i + 2, i) for i in range(count - 2)])
    other = lax.ppermute(own, "cols", swap)
    place = jnp.stack(
        [lax.axis_index("cols"), lax.axis_index("rows"), jnp.asarray(count, jnp.int32)]
    ).astype(jnp.int32)

    code = pl.pallas_call(
        code_kernel,
        out_shape=jax.ShapeDtypeStruct((pairing.shape[0] * pairing.shape[1], width), jnp.int32),
        in_specs=[VMEM],
        out_specs=VMEM,
        compiler_params=PARAMS,
    )(pairing)
    beside = lax.ppermute(
        labels,
        ("rows", "cols"),
        [(2 * (i + 1), 2 * i) for i in range(count - 1)]
        + [(2 * i + 1, 2 * (i + 1) + 1) for i in range(count - 1)],
    )
    gram, turned, own, table = pl.pallas_call(
        local_kernel,
        out_shape=(
            jax.ShapeDtypeStruct((2 * width, width), jnp.float32),
            jax.ShapeDtypeStruct((2 * width, len(THREE) * cells), jnp.bfloat16),
            jax.ShapeDtypeStruct((ny, nz, width), jnp.float32),
            jax.ShapeDtypeStruct((conductivity.shape[0], width), jnp.float32),
        ),
        in_specs=[HBM] * 3 + [VMEM],
        out_specs=[VMEM] * 4,
        scratch_shapes=[
            pltpu.VMEM((cells, width), jnp.float32),
            pltpu.VMEM(labels.shape, jnp.int32),
            pltpu.SMEM(conductivity.shape, jnp.float32),
            pltpu.SemaphoreType.DMA((3,)),
        ],
        compiler_params=PARAMS,
    )(conductivity, own, labels, other)
    beside, table = lax.optimization_barrier((beside, table))
    across = lax.ppermute(beside, "cols", swap)
    kept, sent = pl.pallas_call(
        halo_kernel,
        out_shape=(
            jax.ShapeDtypeStruct((width + 8, width), jnp.float32),
            jax.ShapeDtypeStruct((half, width), jnp.float32),
        ),
        in_specs=[SMEM] + [VMEM] * 7,
        out_specs=[VMEM] * 2,
        scratch_shapes=[pltpu.VMEM((cells, width), jnp.float32)],
        compiler_params=PARAMS,
    )(place, table, own, halo, beside, across, gram, turned)
    received = lax.ppermute(sent, "cols", swap)
    share = jnp.concatenate([kept[: half + 8], kept[half + 8 :] + received], axis=0)
    apart = 1
    while apart < count:
        share = share + lax.ppermute(share, "rows", [(i, i ^ apart) for i in range(count)])
        apart *= 2
    theirs = lax.ppermute(share, "cols", swap)
    rotated, sigma = pl.pallas_call(
        functools.partial(tournament_kernel, pairing.shape[0], pairing.shape[1]),
        out_shape=(
            jax.ShapeDtypeStruct((ny, nz, width), jnp.float32),
            jax.ShapeDtypeStruct((1, width), jnp.float32),
        ),
        in_specs=[SMEM] + [VMEM] * 5,
        out_specs=[VMEM] * 2,
        compiler_params=PARAMS,
    )(place, share, theirs, code, own, other)
    return rotated.reshape(snapshots.shape), sigma.reshape(width)


def solution(mesh):
    placed = (
        P(("groups", "rows"), None, None, "cols"),
        P(("groups", "rows"), None, None),
        P("groups"),
        P(),
    )
    return jax.shard_map(
        shards,
        mesh=mesh,
        in_specs=placed,
        out_specs=(P(("groups", "rows"), None, None, "cols"), P(("groups", "cols"))),
        check_vma=False,
    )
```

```python
import functools

import jax
import jax.numpy as jnp
from jax import lax
from jax.experimental import pallas as pl
from jax.experimental.pallas import tpu as pltpu
from jax.sharding import PartitionSpec as P

PARAMS = pltpu.CompilerParams(vmem_limit_bytes=16 * 2**20)
HBM = pl.BlockSpec(memory_space=pltpu.HBM)
VMEM = pl.BlockSpec(memory_space=pltpu.VMEM)
SMEM = pl.BlockSpec(memory_space=pltpu.SMEM)


def lanes(values, index):
    return jnp.take_along_axis(
        values, jnp.broadcast_to(index, values.shape), axis=1, mode="promise_in_bounds"
    )


def code_kernel(pairing_ref, code_ref):
    meets, turns, n = pairing_ref.shape
    pairs = jnp.concatenate([pairing_ref[m] for m in range(meets)], axis=0)
    place = lax.broadcasted_iota(jnp.int32, pairs.shape, 1)
    told = lanes(pairs, place ^ 1) + jnp.where(place % 2 == 0, n, 0)
    pairs = pairs.astype(jnp.float32).T
    told = told.astype(jnp.float32).T
    col = lax.broadcasted_iota(jnp.int32, (n, n), 1).astype(jnp.float32)
    rows = []
    for index in range(meets * turns):
        here = pairs[:, index : index + 1] == col
        rows.append(jnp.sum(jnp.where(here, told[:, index : index + 1], 0.0), axis=0, keepdims=True))
    code_ref[...] = jnp.concatenate(rows, axis=0).astype(jnp.int32)


def split(values, count):
    parts = []
    for index in range(count):
        part = values.astype(jnp.bfloat16)
        parts.append(part)
        if index < count - 1:
            values = values - part.astype(jnp.float32)
    return parts


TWO = ((0, 0), (0, 1), (1, 0))
THREE = TWO + ((0, 2), (1, 1), (2, 0))


def long_dot(left, right, terms):
    count = 1 + max(i for i, _ in terms)
    left, right = split(left, count), split(right, count)
    return jnp.dot(
        laid(left, terms, 0, 1), laid(right, terms, 1, 0), preferred_element_type=jnp.float32
    )


def laid(parts, terms, side, axis):
    return jnp.concatenate([parts[term[side]] for term in terms], axis=axis)


def column_sums(values):
    return jnp.broadcast_to(jnp.sum(values, axis=0, keepdims=True), (8, values.shape[1]))


def quarter_squares(labels, table):
    squares = jnp.zeros(labels.shape, jnp.float32)
    for region in range(table.shape[0]):
        squares = jnp.where(labels == region, table[region : region + 1, : labels.shape[1]], squares)
    return squares


def local_kernel(
    conductivity_ref, own_hbm_ref, labels_hbm_ref, other_ref,
    gram_ref, turned_ref, own_ref, table_ref,
    applied_ref, labels_ref, regions_ref, sems,
):
    ny, nz, width = own_ref.shape
    cells = ny * nz
    fetches = [
        pltpu.make_async_copy(source, target, sems.at[index])
        for index, (source, target) in enumerate(
            ((own_hbm_ref, own_ref), (labels_hbm_ref, labels_ref), (conductivity_ref, regions_ref))
        )
    ]
    for fetch in fetches:
        fetch.start()
    turned_ref[width:, :] = laid(split(other_ref[...].reshape(cells, width).T, 3), THREE, 0, 1)
    for fetch in fetches:
        fetch.wait()
    table_ref[...] = jnp.concatenate(
        [jnp.full((1, width), 0.25 * regions_ref[region]) for region in range(table_ref.shape[0])],
        axis=0,
    )
    squares = quarter_squares(labels_ref[...], table_ref[...])
    z = lax.broadcasted_iota(jnp.int32, (nz, ny), 0)
    above = jnp.where(z < nz - 1, pltpu.roll(squares, nz - 1, 0), 0.0)
    below = jnp.where(z > 0, pltpu.roll(squares, 1, 0), 0.0)
    inner = 1.0 + above + below
    above = jnp.where(z < nz - 2, above, 0.0)
    below = jnp.where(z > 1, below, 0.0)
    for y in range(ny):
        u = own_ref[y]
        scale = inner[:, y : y + 1]
        if y > 0:
            scale += squares[:, y - 1 : y]
        if y < ny - 1:
            scale += squares[:, y + 1 : y + 2]
        total = scale * u
        if y > 1:
            total -= squares[:, y - 1 : y] * own_ref[y - 2]
        if y < ny - 2:
            total -= squares[:, y + 1 : y + 2] * own_ref[y + 2]
        total -= above[:, y : y + 1] * pltpu.roll(u, nz - 2, 0)
        total -= below[:, y : y + 1] * pltpu.roll(u, 2, 0)
        applied_ref[y * nz : (y + 1) * nz, :] = total
    turned_ref[:width, :] = laid(split(own_ref[...].reshape(cells, width).T, 3), THREE, 0, 1)
    gram_ref[...] = jnp.dot(
        turned_ref[...],
        laid(split(applied_ref[...], 3), THREE, 1, 0),
        preferred_element_type=jnp.float32,
    )


def halo_kernel(
    place_ref, table_ref, own_ref, halo_ref, mine_ref, theirs_ref, gram_ref, turned_ref,
    kept_ref, sent_ref, applied_ref,
):
    ny, nz, width = own_ref.shape
    mine = quarter_squares(mine_ref[...], table_ref[...])
    theirs = quarter_squares(theirs_ref[...], table_ref[...])
    after = jnp.where(place_ref[0] == 0, mine, theirs)
    before = jnp.where(place_ref[0] == 0, theirs, mine)
    after = jnp.where(place_ref[1] < place_ref[2] - 1, after, 0.0)
    before = jnp.where(place_ref[1] > 0, before, 0.0)
    for y in range(ny):
        ahead = after[:, y : y + 1]
        applied_ref[y * nz : (y + 1) * nz, :] = (ahead + before[:, y : y + 1]) * own_ref[y] - (
            2.0 * ahead
        ) * halo_ref[y]
    gram = gram_ref[...] + jnp.dot(
        turned_ref[...],
        laid(split(applied_ref[...], 3), THREE, 1, 0),
        preferred_element_type=jnp.float32,
    )
    half = width // 2
    first = place_ref[0] == 0
    own = gram[:width]
    cross = gram[width:]
    cross = 0.5 * jnp.where(first, cross.T, cross)
    own = 0.5 * (own + own.T)
    row = lax.broadcasted_iota(jnp.int32, (half, width), 0)
    col = lax.broadcasted_iota(jnp.int32, (half, width), 1)
    kept_ref[:half, :] = jnp.where(
        (col >= row), own[:half], pltpu.roll(own[half:], half, 1)
    )
    kept_ref[half : half + 8, :] = column_sums(
        jnp.where(
            lax.broadcasted_iota(jnp.int32, (width, width), 0)
            == lax.broadcasted_iota(jnp.int32, (width, width), 1),
            own,
            0.0,
        )
    )
    kept_ref[half + 8 :, :] = jnp.where(first, cross[:half], cross[half:])
    sent_ref[...] = jnp.where(first, cross[half:], cross[:half])


def unpacked(share):
    n = share.shape[1]
    h = n // 2
    top = share[:h]
    row = lax.broadcasted_iota(jnp.int32, (h, n), 0)
    col = lax.broadcasted_iota(jnp.int32, (h, n), 1)
    mirror = top.T
    wide = jnp.concatenate([mirror[:h], mirror[:h]], axis=1)
    first = jnp.where(col >= row, top, wide)
    second = jnp.where(col - h < row, pltpu.roll(top, h, 1), wide)
    second = jnp.where(col - h == row, share[h : h + 1], second)
    tall = jnp.concatenate([mirror[h:], mirror[h:]], axis=1)
    return jnp.concatenate([first, jnp.where(col < h, tall, second)], axis=0)


def rotation(diagonal, opposite, coupling, first):
    g_first = jnp.where(first, diagonal, opposite)
    g_second = jnp.where(first, opposite, diagonal)
    spread = g_first - g_second
    radius = jnp.sqrt(spread * spread + 4.0 * coupling * coupling)
    turned = jnp.where(spread > 0, -2.0, jnp.where(spread < 0, 2.0, 0.0)) * coupling
    tangent = turned * pl.reciprocal(
        jnp.abs(spread) + radius + 1e-06 * (g_first + g_second + 1.0), approx=False
    )
    cosine = lax.rsqrt(1.0 + tangent * tangent)
    sine = cosine * tangent
    return cosine, jnp.where(first, -sine, sine)


def tournament_kernel(
    meets, turns, place_ref, mine_ref, theirs_ref, code_ref, own_ref, other_ref, rotated_ref, sigma_ref
):
    n = own_ref.shape[2]
    h = n // 2
    side = place_ref[0] == 0
    mine, theirs = mine_ref[...], theirs_ref[...]
    zero_side = jnp.where(side, mine, theirs)
    one_side = jnp.where(side, theirs, mine)
    eye = lax.broadcasted_iota(jnp.int32, (n, n), 0) == lax.broadcasted_iota(jnp.int32, (n, n), 1)
    blank = jnp.zeros((n, n), jnp.float32)
    low_half = lax.broadcasted_iota(jnp.int32, (h, n), 1) < h
    low = lax.broadcasted_iota(jnp.int32, (2 * n, n), 1) < h

    tiles = range(n // 8)
    rows = [lax.broadcasted_iota(jnp.int32, (8, n), 0) + 8 * i for i in tiles]
    cols = lax.broadcasted_iota(jnp.int32, (8, n), 1)
    near = [unpacked(zero_side), unpacked(one_side)]
    cross = jnp.concatenate([zero_side[h + 8 :], one_side[h + 8 :]], axis=0)
    diagonal = [column_sums(jnp.where(eye, near[d], 0.0)) for d in range(2)]
    total = None
    slots = [[0, 1], [2, 3]]
    upper, lower = [0, 2], [1, 3]
    for meeting in range(meets):
        last = meeting == meets - 1
        uppers = {frozenset((upper[d], lower[d])): upper[d] for d in range(2)}
        swapped = [uppers[frozenset(slots[d])] != slots[d][0] for d in range(2)]
        factor = [None, None]
        near = [[near[d][8 * i : 8 * i + 8] for i in tiles] for d in range(2)]
        cross = [cross[8 * i : 8 * i + 8] for i in tiles]
        for turn in range(turns):
            index = meeting * turns + turn
            told = jnp.broadcast_to(code_ref[index : index + 1, :], (8, n))
            other_way = pltpu.roll(told, h, 1)
            for d in range(2):
                partner = (other_way % n) ^ h if swapped[d] else told % n
                first = (other_way if swapped[d] else told) >= n
                if turn == 0:
                    coupling = [
                        jnp.where(rows[i] == partner, near[d][i], 0.0) for i in tiles
                    ]
                else:
                    opposite = [lanes(part, partner) for part in factor[d]]
                    coupling = [left * right for left, right in zip(opposite, near[d])]
                while len(coupling) > 1:
                    coupling = [a + b for a, b in zip(coupling[::2], coupling[1::2])]
                coupling = column_sums(coupling[0])
                across = lanes(diagonal[d], partner)
                cosine, sine = rotation(diagonal[d], across, coupling, first)
                diagonal[d] = (
                    cosine * cosine * diagonal[d] + 2.0 * cosine * sine * coupling + sine * sine * across
                )
                if turn == 0:
                    factor[d] = [
                        jnp.where(rows[i] == cols, cosine, jnp.where(rows[i] == partner, sine, 0.0))
                        for i in tiles
                    ]
                else:
                    factor[d] = [
                        part * cosine + away * sine for part, away in zip(factor[d], opposite)
                    ]
                if not last or turn < turns - 1:
                    near[d] = [part * cosine + lanes(part, partner) * sine for part in near[d]]
                if not last and d == 1:
                    cross = [part * cosine + lanes(part, partner) * sine for part in cross]
        factor = [jnp.concatenate(factor[d], axis=0) for d in range(2)]
        if last:
            break
        if total is None:
            total = [
                jnp.concatenate([factor[0], blank], axis=0),
                jnp.concatenate([blank, factor[1]], axis=0),
            ]
        else:
            total = [long_dot(total[d], factor[d], TWO) for d in range(2)]
        near = [jnp.concatenate(near[d], axis=0) for d in range(2)]
        cross = jnp.concatenate(cross, axis=0)
        top = long_dot(factor[0].T, jnp.concatenate([near[0], cross], axis=1), THREE)
        g00, g01 = top[:, :n], top[:, n:]
        g11 = long_dot(factor[1].T, near[1], THREE)
        g10 = g01.T
        upper, lower = [upper[0], lower[0]], [lower[1], upper[1]]
        meets_next = [frozenset((upper[d], lower[d])) for d in range(2)]
        if frozenset((slots[0][0], slots[1][1])) not in meets_next:
            slots[1] = slots[1][::-1]
            g01, g11 = pltpu.roll(g01, h, 1), pltpu.roll(g11, h, 1)
            g10 = jnp.concatenate([g10[h:], g10[:h]], axis=0)
            g11 = jnp.concatenate([g11[h:], g11[:h]], axis=0)
            total[1] = pltpu.roll(total[1], h, 1)
            diagonal[1] = pltpu.roll(diagonal[1], h, 1)
        slots = [[slots[0][0], slots[1][1]], [slots[1][0], slots[0][1]]]

        def mixed(first, second, third, fourth):
            return jnp.concatenate(
                [
                    jnp.where(low_half, first[:h], second[:h]),
                    jnp.where(low_half, third[h:], fourth[h:]),
                ],
                axis=0,
            )

        near = [mixed(g00, g01, g10, g11), mixed(g11, g10, g01, g00)]
        cross = mixed(g01, g00, g11, g10)
        diagonal = [
            jnp.where(cols < h, diagonal[0], diagonal[1]),
            jnp.where(cols < h, diagonal[1], diagonal[0]),
        ]
        total = [jnp.where(low, total[0], total[1]), jnp.where(low, total[1], total[0])]

    flat = jnp.concatenate(
        [own_ref[...].reshape(-1, n), other_ref[...].reshape(-1, n)], axis=1
    )
    both = jnp.concatenate(total, axis=1)
    both = jnp.concatenate(
        [jnp.where(side, both[:n], both[n:]), jnp.where(side, both[n:], both[:n])], axis=0
    )
    before_last = long_dot(flat, both, TWO)
    gap = jnp.zeros((n, h), jnp.float32)
    blocks, norms = {}, {}
    for d in range(2):
        norm = jnp.sqrt(diagonal[d][:1])
        for i in range(2):
            part = factor[d][:, i * h : (i + 1) * h]
            blocks[slots[d][i]] = jnp.concatenate([part, gap] if d == 0 else [gap, part], axis=0)
            norms[slots[d][i]] = norm[:, i * h : (i + 1) * h]
    picked = jnp.where(
        side,
        jnp.concatenate([blocks[0], blocks[1]], axis=1),
        jnp.concatenate([blocks[2], blocks[3]], axis=1),
    )
    rotated_ref[...] = long_dot(before_last, picked, TWO).reshape(rotated_ref.shape)
    sigma_ref[...] = jnp.where(
        side,
        jnp.concatenate([norms[0], norms[1]], axis=1),
        jnp.concatenate([norms[2], norms[3]], axis=1),
    )


def shards(snapshots, labels, conductivity, pairing):
    planes, ny, nz, width = snapshots.shape
    cells = planes * ny * nz
    half = width // 2
    count = lax.axis_size("rows")
    swap = [(0, 1), (1, 0)]
    own = snapshots[0]
    labels = labels[0].T
    halo = lax.ppermute(own, "rows", [(i + 2, i) for i in range(count - 2)])
    other = lax.ppermute(own, "cols", swap)
    place = jnp.stack(
        [lax.axis_index("cols"), lax.axis_index("rows"), jnp.asarray(count, jnp.int32)]
    ).astype(jnp.int32)

    code = pl.pallas_call(
        code_kernel,
        out_shape=jax.ShapeDtypeStruct((pairing.shape[0] * pairing.shape[1], width), jnp.int32),
        in_specs=[VMEM],
        out_specs=VMEM,
        compiler_params=PARAMS,
    )(pairing)
    beside = lax.ppermute(
        labels,
        ("rows", "cols"),
        [(2 * (i + 1), 2 * i) for i in range(count - 1)]
        + [(2 * i + 1, 2 * (i + 1) + 1) for i in range(count - 1)],
    )
    gram, turned, own, table = pl.pallas_call(
        local_kernel,
        out_shape=(
            jax.ShapeDtypeStruct((2 * width, width), jnp.float32),
            jax.ShapeDtypeStruct((2 * width, len(THREE) * cells), jnp.bfloat16),
            jax.ShapeDtypeStruct((ny, nz, width), jnp.float32),
            jax.ShapeDtypeStruct((conductivity.shape[0], width), jnp.float32),
        ),
        in_specs=[HBM] * 3 + [VMEM],
        out_specs=[VMEM] * 4,
        scratch_shapes=[
            pltpu.VMEM((cells, width), jnp.float32),
            pltpu.VMEM(labels.shape, jnp.int32),
            pltpu.SMEM(conductivity.shape, jnp.float32),
            pltpu.SemaphoreType.DMA((3,)),
        ],
        compiler_params=PARAMS,
    )(*[pltpu.with_memory_space_constraint(value, pltpu.HBM) for value in (conductivity, own, labels)], other)
    beside, table = lax.optimization_barrier((beside, table))
    across = lax.ppermute(beside, "cols", swap)
    kept, sent = pl.pallas_call(
        halo_kernel,
        out_shape=(
            jax.ShapeDtypeStruct((width + 8, width), jnp.float32),
            jax.ShapeDtypeStruct((half, width), jnp.float32),
        ),
        in_specs=[SMEM] + [VMEM] * 7,
        out_specs=[VMEM] * 2,
        scratch_shapes=[pltpu.VMEM((cells, width), jnp.float32)],
        compiler_params=PARAMS,
    )(place, table, own, halo, beside, across, gram, turned)
    received = lax.ppermute(sent, "cols", swap)
    share = jnp.concatenate([kept[: half + 8], kept[half + 8 :] + received], axis=0)
    apart = 1
    while apart < count:
        share = share + lax.ppermute(share, "rows", [(i, i ^ apart) for i in range(count)])
        apart *= 2
    theirs = lax.ppermute(share, "cols", swap)
    rotated, sigma = pl.pallas_call(
        functools.partial(tournament_kernel, pairing.shape[0], pairing.shape[1]),
        out_shape=(
            jax.ShapeDtypeStruct((ny, nz, width), jnp.float32),
            jax.ShapeDtypeStruct((1, width), jnp.float32),
        ),
        in_specs=[SMEM] + [VMEM] * 5,
        out_specs=[VMEM] * 2,
        compiler_params=PARAMS,
    )(place, share, theirs, code, own, other)
    return rotated.reshape(snapshots.shape), sigma.reshape(width)


def solution(mesh):
    placed = (
        P(("groups", "rows"), None, None, "cols"),
        P(("groups", "rows"), None, None),
        P("groups"),
        P(),
    )
    return jax.shard_map(
        shards,
        mesh=mesh,
        in_specs=placed,
        out_specs=(P(("groups", "rows"), None, None, "cols"), P(("groups", "cols"))),
        check_vma=False,
    )
```

```python
import functools

import jax
import jax.numpy as jnp
from jax import lax
from jax.experimental import pallas as pl
from jax.experimental.pallas import tpu as pltpu
from jax.sharding import PartitionSpec as P

PARAMS = pltpu.CompilerParams(vmem_limit_bytes=16 * 2**20)
HBM = pl.BlockSpec(memory_space=pltpu.HBM)
VMEM = pl.BlockSpec(memory_space=pltpu.VMEM)
SMEM = pl.BlockSpec(memory_space=pltpu.SMEM)


def lanes(values, index):
    return jnp.take_along_axis(
        values, jnp.broadcast_to(index, values.shape), axis=1, mode="promise_in_bounds"
    )


def code_kernel(pairing_ref, code_ref):
    meets, turns, n = pairing_ref.shape
    pairs = jnp.concatenate([pairing_ref[m] for m in range(meets)], axis=0)
    place = lax.broadcasted_iota(jnp.int32, pairs.shape, 1)
    told = lanes(pairs, place ^ 1) + jnp.where(place % 2 == 0, n, 0)
    pairs = pairs.astype(jnp.float32).T
    told = told.astype(jnp.float32).T
    col = lax.broadcasted_iota(jnp.int32, (n, n), 1).astype(jnp.float32)
    rows = []
    for index in range(meets * turns):
        here = pairs[:, index : index + 1] == col
        rows.append(jnp.sum(jnp.where(here, told[:, index : index + 1], 0.0), axis=0, keepdims=True))
    code_ref[...] = jnp.concatenate(rows, axis=0).astype(jnp.int32)


def split(values, count):
    parts = []
    for index in range(count):
        part = values.astype(jnp.bfloat16)
        parts.append(part)
        if index < count - 1:
            values = values - part.astype(jnp.float32)
    return parts


TWO = ((0, 0), (0, 1), (1, 0))
THREE = TWO + ((0, 2), (1, 1), (2, 0))


def long_dot(left, right, terms):
    count = 1 + max(i for i, _ in terms)
    left, right = split(left, count), split(right, count)
    return jnp.dot(
        laid(left, terms, 0, 1), laid(right, terms, 1, 0), preferred_element_type=jnp.float32
    )


def laid(parts, terms, side, axis):
    return jnp.concatenate([parts[term[side]] for term in terms], axis=axis)


def column_sums(values):
    return jnp.broadcast_to(jnp.sum(values, axis=0, keepdims=True), (8, values.shape[1]))


def quarter_squares(labels, table):
    squares = jnp.zeros(labels.shape, jnp.float32)
    for region in range(table.shape[0]):
        squares = jnp.where(labels == region, table[region : region + 1, : labels.shape[1]], squares)
    return squares


def local_kernel(
    conductivity_ref, own_hbm_ref, labels_hbm_ref, other_ref,
    gram_ref, turned_ref, own_ref, table_ref,
    applied_ref, labels_ref, regions_ref, sems,
):
    ny, nz, width = own_ref.shape
    cells = ny * nz
    fetches = [
        pltpu.make_async_copy(source, target, sems.at[index])
        for index, (source, target) in enumerate(
            ((own_hbm_ref, own_ref), (labels_hbm_ref, labels_ref), (conductivity_ref, regions_ref))
        )
    ]
    for fetch in fetches:
        fetch.start()
    turned_ref[width:, :] = laid(split(other_ref[...].reshape(cells, width).T, 3), THREE, 0, 1)
    for fetch in fetches:
        fetch.wait()
    table_ref[...] = jnp.concatenate(
        [jnp.full((1, width), 0.25 * regions_ref[region]) for region in range(table_ref.shape[0])],
        axis=0,
    )
    squares = quarter_squares(labels_ref[...], table_ref[...])
    z = lax.broadcasted_iota(jnp.int32, (nz, ny), 0)
    above = jnp.where(z < nz - 1, pltpu.roll(squares, nz - 1, 0), 0.0)
    below = jnp.where(z > 0, pltpu.roll(squares, 1, 0), 0.0)
    inner = 1.0 + above + below
    above = jnp.where(z < nz - 2, above, 0.0)
    below = jnp.where(z > 1, below, 0.0)
    for y in range(ny):
        u = own_ref[y]
        scale = inner[:, y : y + 1]
        if y > 0:
            scale += squares[:, y - 1 : y]
        if y < ny - 1:
            scale += squares[:, y + 1 : y + 2]
        total = scale * u
        if y > 1:
            total -= squares[:, y - 1 : y] * own_ref[y - 2]
        if y < ny - 2:
            total -= squares[:, y + 1 : y + 2] * own_ref[y + 2]
        total -= above[:, y : y + 1] * pltpu.roll(u, nz - 2, 0)
        total -= below[:, y : y + 1] * pltpu.roll(u, 2, 0)
        applied_ref[y * nz : (y + 1) * nz, :] = total
    turned_ref[:width, :] = laid(split(own_ref[...].reshape(cells, width).T, 3), THREE, 0, 1)
    gram_ref[...] = jnp.dot(
        turned_ref[...],
        laid(split(applied_ref[...], 3), THREE, 1, 0),
        preferred_element_type=jnp.float32,
    )


def halo_kernel(
    place_ref, table_ref, own_ref, halo_ref, mine_ref, theirs_ref, gram_ref, turned_ref,
    parts_ref, cross_ref, sent_ref, applied_ref,
):
    ny, nz, width = own_ref.shape
    mine = quarter_squares(mine_ref[...], table_ref[...])
    theirs = quarter_squares(theirs_ref[...], table_ref[...])
    ahead_first = place_ref[0] == place_ref[1] % 2
    after = jnp.where(ahead_first, mine, theirs)
    before = jnp.where(ahead_first, theirs, mine)
    after = jnp.where(place_ref[1] < place_ref[2] - 1, after, 0.0)
    before = jnp.where(place_ref[1] > 0, before, 0.0)
    around = after + before
    after = 2.0 * after
    for y in range(ny):
        applied_ref[y * nz : (y + 1) * nz, :] = (
            around[:, y : y + 1] * own_ref[y] - after[:, y : y + 1] * halo_ref[y]
        )
    parts = laid(split(applied_ref[...], 3), THREE, 1, 0)
    parts_ref[...] = parts
    half = width // 2
    first = place_ref[0] == 0
    cross = gram_ref[width:, :] + jnp.dot(
        turned_ref[width:, :], parts, preferred_element_type=jnp.float32
    )
    cross = 0.5 * jnp.where(first, cross.T, cross)
    cross_ref[...] = jnp.where(first, cross[:half], cross[half:])
    sent_ref[...] = jnp.where(first, cross[half:], cross[:half])


def own_kernel(gram_ref, turned_ref, parts_ref, packed_ref):
    width = parts_ref.shape[1]
    half = width // 2
    own = gram_ref[:width, :] + jnp.dot(
        turned_ref[:width, :], parts_ref[...], preferred_element_type=jnp.float32
    )
    own = 0.5 * (own + own.T)
    row = lax.broadcasted_iota(jnp.int32, (half, width), 0)
    col = lax.broadcasted_iota(jnp.int32, (half, width), 1)
    packed_ref[:half, :] = jnp.where(col >= row, own[:half], pltpu.roll(own[half:], half, 1))
    packed_ref[half:, :] = column_sums(
        jnp.where(
            lax.broadcasted_iota(jnp.int32, (width, width), 0)
            == lax.broadcasted_iota(jnp.int32, (width, width), 1),
            own,
            0.0,
        )
    )


def unpacked(share):
    n = share.shape[1]
    h = n // 2
    top = share[:h]
    row = lax.broadcasted_iota(jnp.int32, (h, n), 0)
    col = lax.broadcasted_iota(jnp.int32, (h, n), 1)
    mirror = top.T
    wide = jnp.concatenate([mirror[:h], mirror[:h]], axis=1)
    first = jnp.where(col >= row, top, wide)
    second = jnp.where(col - h < row, pltpu.roll(top, h, 1), wide)
    second = jnp.where(col - h == row, share[h : h + 1], second)
    tall = jnp.concatenate([mirror[h:], mirror[h:]], axis=1)
    return jnp.concatenate([first, jnp.where(col < h, tall, second)], axis=0)


def rotation(diagonal, opposite, coupling, first):
    g_first = jnp.where(first, diagonal, opposite)
    g_second = jnp.where(first, opposite, diagonal)
    spread = g_first - g_second
    radius = jnp.sqrt(spread * spread + 4.0 * coupling * coupling)
    turned = jnp.where(spread > 0, -2.0, jnp.where(spread < 0, 2.0, 0.0)) * coupling
    tangent = turned * pl.reciprocal(
        jnp.abs(spread) + radius + 1e-06 * (g_first + g_second + 1.0), approx=False
    )
    cosine = lax.rsqrt(1.0 + tangent * tangent)
    sine = cosine * tangent
    return cosine, jnp.where(first, -sine, sine)


def tournament_kernel(
    meets, turns, place_ref, mine_ref, theirs_ref, code_ref, own_ref, other_ref, rotated_ref, sigma_ref
):
    n = own_ref.shape[2]
    h = n // 2
    side = place_ref[0] == 0
    mine, theirs = mine_ref[...], theirs_ref[...]
    zero_side = jnp.where(side, mine, theirs)
    one_side = jnp.where(side, theirs, mine)
    eye = lax.broadcasted_iota(jnp.int32, (n, n), 0) == lax.broadcasted_iota(jnp.int32, (n, n), 1)
    blank = jnp.zeros((n, n), jnp.float32)
    low_half = lax.broadcasted_iota(jnp.int32, (h, n), 1) < h
    low = lax.broadcasted_iota(jnp.int32, (2 * n, n), 1) < h

    tiles = range(n // 8)
    rows = [lax.broadcasted_iota(jnp.int32, (8, n), 0) + 8 * i for i in tiles]
    cols = lax.broadcasted_iota(jnp.int32, (8, n), 1)
    near = [unpacked(zero_side), unpacked(one_side)]
    cross = jnp.concatenate([zero_side[h + 8 :], one_side[h + 8 :]], axis=0)
    diagonal = [column_sums(jnp.where(eye, near[d], 0.0)) for d in range(2)]
    total = None
    slots = [[0, 1], [2, 3]]
    upper, lower = [0, 2], [1, 3]
    for meeting in range(meets):
        last = meeting == meets - 1
        uppers = {frozenset((upper[d], lower[d])): upper[d] for d in range(2)}
        swapped = [uppers[frozenset(slots[d])] != slots[d][0] for d in range(2)]
        factor = [None, None]
        near = [[near[d][8 * i : 8 * i + 8] for i in tiles] for d in range(2)]
        cross = [cross[8 * i : 8 * i + 8] for i in tiles]
        for turn in range(turns):
            index = meeting * turns + turn
            told = jnp.broadcast_to(code_ref[index : index + 1, :], (8, n))
            other_way = pltpu.roll(told, h, 1)
            for d in range(2):
                partner = (other_way % n) ^ h if swapped[d] else told % n
                first = (other_way if swapped[d] else told) >= n
                if turn == 0:
                    coupling = [
                        jnp.where(rows[i] == partner, near[d][i], 0.0) for i in tiles
                    ]
                else:
                    opposite = [lanes(part, partner) for part in factor[d]]
                    coupling = [left * right for left, right in zip(opposite, near[d])]
                while len(coupling) > 1:
                    coupling = [a + b for a, b in zip(coupling[::2], coupling[1::2])]
                coupling = column_sums(coupling[0])
                across = lanes(diagonal[d], partner)
                cosine, sine = rotation(diagonal[d], across, coupling, first)
                diagonal[d] = (
                    cosine * cosine * diagonal[d] + 2.0 * cosine * sine * coupling + sine * sine * across
                )
                if turn == 0:
                    factor[d] = [
                        jnp.where(rows[i] == cols, cosine, jnp.where(rows[i] == partner, sine, 0.0))
                        for i in tiles
                    ]
                else:
                    factor[d] = [
                        part * cosine + away * sine for part, away in zip(factor[d], opposite)
                    ]
                if not last or turn < turns - 1:
                    near[d] = [part * cosine + lanes(part, partner) * sine for part in near[d]]
                if not last and d == 1:
                    cross = [part * cosine + lanes(part, partner) * sine for part in cross]
        factor = [jnp.concatenate(factor[d], axis=0) for d in range(2)]
        if last:
            break
        if total is None:
            total = [
                jnp.concatenate([factor[0], blank], axis=0),
                jnp.concatenate([blank, factor[1]], axis=0),
            ]
        else:
            total = [long_dot(total[d], factor[d], TWO) for d in range(2)]
        near = [jnp.concatenate(near[d], axis=0) for d in range(2)]
        cross = jnp.concatenate(cross, axis=0)
        top = long_dot(factor[0].T, jnp.concatenate([near[0], cross], axis=1), THREE)
        g00, g01 = top[:, :n], top[:, n:]
        g11 = long_dot(factor[1].T, near[1], THREE)
        g10 = g01.T
        upper, lower = [upper[0], lower[0]], [lower[1], upper[1]]
        meets_next = [frozenset((upper[d], lower[d])) for d in range(2)]
        if frozenset((slots[0][0], slots[1][1])) not in meets_next:
            slots[1] = slots[1][::-1]
            g01, g11 = pltpu.roll(g01, h, 1), pltpu.roll(g11, h, 1)
            g10 = jnp.concatenate([g10[h:], g10[:h]], axis=0)
            g11 = jnp.concatenate([g11[h:], g11[:h]], axis=0)
            total[1] = pltpu.roll(total[1], h, 1)
            diagonal[1] = pltpu.roll(diagonal[1], h, 1)
        slots = [[slots[0][0], slots[1][1]], [slots[1][0], slots[0][1]]]

        def mixed(first, second, third, fourth):
            return jnp.concatenate(
                [
                    jnp.where(low_half, first[:h], second[:h]),
                    jnp.where(low_half, third[h:], fourth[h:]),
                ],
                axis=0,
            )

        near = [mixed(g00, g01, g10, g11), mixed(g11, g10, g01, g00)]
        cross = mixed(g01, g00, g11, g10)
        diagonal = [
            jnp.where(cols < h, diagonal[0], diagonal[1]),
            jnp.where(cols < h, diagonal[1], diagonal[0]),
        ]
        total = [jnp.where(low, total[0], total[1]), jnp.where(low, total[1], total[0])]

    flat = jnp.concatenate(
        [own_ref[...].reshape(-1, n), other_ref[...].reshape(-1, n)], axis=1
    )
    both = jnp.concatenate(total, axis=1)
    both = jnp.concatenate(
        [jnp.where(side, both[:n], both[n:]), jnp.where(side, both[n:], both[:n])], axis=0
    )
    before_last = long_dot(flat, both, TWO)
    gap = jnp.zeros((n, h), jnp.float32)
    blocks, norms = {}, {}
    for d in range(2):
        norm = jnp.sqrt(diagonal[d][:1])
        for i in range(2):
            part = factor[d][:, i * h : (i + 1) * h]
            blocks[slots[d][i]] = jnp.concatenate([part, gap] if d == 0 else [gap, part], axis=0)
            norms[slots[d][i]] = norm[:, i * h : (i + 1) * h]
    picked = jnp.where(
        side,
        jnp.concatenate([blocks[0], blocks[1]], axis=1),
        jnp.concatenate([blocks[2], blocks[3]], axis=1),
    )
    rotated_ref[...] = long_dot(before_last, picked, TWO).reshape(rotated_ref.shape)
    sigma_ref[...] = jnp.where(
        side,
        jnp.concatenate([norms[0], norms[1]], axis=1),
        jnp.concatenate([norms[2], norms[3]], axis=1),
    )


def shards(snapshots, labels, conductivity, pairing):
    planes, ny, nz, width = snapshots.shape
    cells = planes * ny * nz
    half = width // 2
    count = lax.axis_size("rows")
    swap = [(0, 1), (1, 0)]
    own = snapshots[0]
    labels = labels[0].T
    halo = lax.ppermute(own, "rows", [(i + 2, i) for i in range(count - 2)])
    other = lax.ppermute(own, "cols", swap)
    place = jnp.stack(
        [lax.axis_index("cols"), lax.axis_index("rows"), jnp.asarray(count, jnp.int32)]
    ).astype(jnp.int32)

    code = pl.pallas_call(
        code_kernel,
        out_shape=jax.ShapeDtypeStruct((pairing.shape[0] * pairing.shape[1], width), jnp.int32),
        in_specs=[VMEM],
        out_specs=VMEM,
        compiler_params=PARAMS,
    )(pairing)
    beside = lax.ppermute(
        labels,
        ("rows", "cols"),
        [(2 * i, 2 * (i ^ 1)) for i in range(count)]
        + [(2 * i + 1, 2 * (i + (1 if i % 2 else -1)) + 1) for i in range(1, count - 1)],
    )
    gram, turned, own, table = pl.pallas_call(
        local_kernel,
        out_shape=(
            jax.ShapeDtypeStruct((2 * width, width), jnp.float32),
            jax.ShapeDtypeStruct((2 * width, len(THREE) * cells), jnp.bfloat16),
            jax.ShapeDtypeStruct((ny, nz, width), jnp.float32),
            jax.ShapeDtypeStruct((conductivity.shape[0], width), jnp.float32),
        ),
        in_specs=[HBM] * 3 + [VMEM],
        out_specs=[VMEM] * 4,
        scratch_shapes=[
            pltpu.VMEM((cells, width), jnp.float32),
            pltpu.VMEM(labels.shape, jnp.int32),
            pltpu.SMEM(conductivity.shape, jnp.float32),
            pltpu.SemaphoreType.DMA((3,)),
        ],
        compiler_params=PARAMS,
    )(*[pltpu.with_memory_space_constraint(value, pltpu.HBM) for value in (conductivity, own, labels)], other)
    beside, table = lax.optimization_barrier((beside, table))
    across = lax.ppermute(beside, "cols", swap)
    parts, cross, sent = pl.pallas_call(
        halo_kernel,
        out_shape=(
            jax.ShapeDtypeStruct((len(THREE) * cells, width), jnp.bfloat16),
            jax.ShapeDtypeStruct((half, width), jnp.float32),
            jax.ShapeDtypeStruct((half, width), jnp.float32),
        ),
        in_specs=[SMEM] + [VMEM] * 7,
        out_specs=[VMEM] * 3,
        scratch_shapes=[pltpu.VMEM((cells, width), jnp.float32)],
        compiler_params=PARAMS,
    )(place, table, own, halo, beside, across, gram, turned)
    received = lax.ppermute(sent, "cols", swap)
    packed = pl.pallas_call(
        own_kernel,
        out_shape=jax.ShapeDtypeStruct((half + 8, width), jnp.float32),
        in_specs=[VMEM] * 3,
        out_specs=VMEM,
        compiler_params=PARAMS,
    )(gram, turned, parts)
    share = jnp.concatenate([packed, cross + received], axis=0)
    apart = 1
    while apart < count:
        share = share + lax.ppermute(share, "rows", [(i, i ^ apart) for i in range(count)])
        apart *= 2
    theirs = lax.ppermute(share, "cols", swap)
    rotated, sigma = pl.pallas_call(
        functools.partial(tournament_kernel, pairing.shape[0], pairing.shape[1]),
        out_shape=(
            jax.ShapeDtypeStruct((ny, nz, width), jnp.float32),
            jax.ShapeDtypeStruct((1, width), jnp.float32),
        ),
        in_specs=[SMEM] + [VMEM] * 5,
        out_specs=[VMEM] * 2,
        compiler_params=PARAMS,
    )(place, share, theirs, code, own, other)
    return rotated.reshape(snapshots.shape), sigma.reshape(width)


def solution(mesh):
    placed = (
        P(("groups", "rows"), None, None, "cols"),
        P(("groups", "rows"), None, None),
        P("groups"),
        P(),
    )
    return jax.shard_map(
        shards,
        mesh=mesh,
        in_specs=placed,
        out_specs=(P(("groups", "rows"), None, None, "cols"), P(("groups", "cols"))),
        check_vma=False,
    )
```

```python
import functools

import jax
import jax.numpy as jnp
from jax import lax
from jax.experimental import pallas as pl
from jax.experimental.pallas import tpu as pltpu
from jax.sharding import PartitionSpec as P

PARAMS = pltpu.CompilerParams(vmem_limit_bytes=16 * 2**20)
HBM = pl.BlockSpec(memory_space=pltpu.HBM)
VMEM = pl.BlockSpec(memory_space=pltpu.VMEM)
SMEM = pl.BlockSpec(memory_space=pltpu.SMEM)


def lanes(values, index):
    return jnp.take_along_axis(
        values, jnp.broadcast_to(index, values.shape), axis=1, mode="promise_in_bounds"
    )


def code_kernel(pairing_ref, code_ref):
    meets, turns, n = pairing_ref.shape
    pairs = jnp.concatenate([pairing_ref[m] for m in range(meets)], axis=0)
    place = lax.broadcasted_iota(jnp.int32, pairs.shape, 1)
    told = lanes(pairs, place ^ 1) + jnp.where(place % 2 == 0, n, 0)
    pairs = pairs.astype(jnp.float32).T
    told = told.astype(jnp.float32).T
    col = lax.broadcasted_iota(jnp.int32, (n, n), 1).astype(jnp.float32)
    rows = []
    for index in range(meets * turns):
        here = pairs[:, index : index + 1] == col
        rows.append(jnp.sum(jnp.where(here, told[:, index : index + 1], 0.0), axis=0, keepdims=True))
    code_ref[...] = jnp.concatenate(rows, axis=0).astype(jnp.int32)


def split(values, count):
    parts = []
    for index in range(count):
        part = values.astype(jnp.bfloat16)
        parts.append(part)
        if index < count - 1:
            values = values - part.astype(jnp.float32)
    return parts


TWO = ((0, 0), (0, 1), (1, 0))
THREE = TWO + ((0, 2), (1, 1), (2, 0))


def long_dot(left, right, terms):
    count = 1 + max(i for i, _ in terms)
    left, right = split(left, count), split(right, count)
    return jnp.dot(
        laid(left, terms, 0, 1), laid(right, terms, 1, 0), preferred_element_type=jnp.float32
    )


def laid(parts, terms, side, axis):
    return jnp.concatenate([parts[term[side]] for term in terms], axis=axis)


def column_sums(values):
    return jnp.broadcast_to(jnp.sum(values, axis=0, keepdims=True), (8, values.shape[1]))


def quarter_squares(labels, table):
    squares = jnp.zeros(labels.shape, jnp.float32)
    for region in range(table.shape[0]):
        squares = jnp.where(labels == region, table[region : region + 1, : labels.shape[1]], squares)
    return squares


def local_kernel(
    conductivity_ref, own_hbm_ref, labels_hbm_ref, other_ref,
    gram_ref, turned_ref, own_ref, table_ref,
    applied_ref, labels_ref, regions_ref, sems,
):
    ny, nz, width = own_ref.shape
    cells = ny * nz
    fetches = [
        pltpu.make_async_copy(source, target, sems.at[index])
        for index, (source, target) in enumerate(
            ((own_hbm_ref, own_ref), (labels_hbm_ref, labels_ref), (conductivity_ref, regions_ref))
        )
    ]
    for fetch in fetches:
        fetch.start()
    turned_ref[width:, :] = laid(split(other_ref[...].reshape(cells, width).T, 3), THREE, 0, 1)
    for fetch in fetches:
        fetch.wait()
    table_ref[...] = jnp.concatenate(
        [jnp.full((1, width), 0.25 * regions_ref[region]) for region in range(table_ref.shape[0])],
        axis=0,
    )
    squares = quarter_squares(labels_ref[...], table_ref[...])
    z = lax.broadcasted_iota(jnp.int32, (nz, ny), 0)
    above = jnp.where(z < nz - 1, pltpu.roll(squares, nz - 1, 0), 0.0)
    below = jnp.where(z > 0, pltpu.roll(squares, 1, 0), 0.0)
    inner = 1.0 + above + below
    above = jnp.where(z < nz - 2, above, 0.0)
    below = jnp.where(z > 1, below, 0.0)
    for y in range(ny):
        u = own_ref[y]
        scale = inner[:, y : y + 1]
        if y > 0:
            scale += squares[:, y - 1 : y]
        if y < ny - 1:
            scale += squares[:, y + 1 : y + 2]
        total = scale * u
        if y > 1:
            total -= squares[:, y - 1 : y] * own_ref[y - 2]
        if y < ny - 2:
            total -= squares[:, y + 1 : y + 2] * own_ref[y + 2]
        total -= above[:, y : y + 1] * pltpu.roll(u, nz - 2, 0)
        total -= below[:, y : y + 1] * pltpu.roll(u, 2, 0)
        applied_ref[y * nz : (y + 1) * nz, :] = total
    turned_ref[:width, :] = laid(split(own_ref[...].reshape(cells, width).T, 3), THREE, 0, 1)
    gram_ref[...] = jnp.dot(
        turned_ref[...],
        laid(split(applied_ref[...], 3), THREE, 1, 0),
        preferred_element_type=jnp.float32,
    )


def halo_kernel(
    place_ref, table_ref, own_ref, halo_ref, mine_ref, theirs_ref, gram_ref, turned_ref,
    parts_ref, cross_ref, sent_ref, applied_ref,
):
    ny, nz, width = own_ref.shape
    mine = quarter_squares(mine_ref[...], table_ref[...])
    theirs = quarter_squares(theirs_ref[...], table_ref[...])
    ahead_first = place_ref[0] == place_ref[1] % 2
    after = jnp.where(ahead_first, mine, theirs)
    before = jnp.where(ahead_first, theirs, mine)
    after = jnp.where(place_ref[1] < place_ref[2] - 1, after, 0.0)
    before = jnp.where(place_ref[1] > 0, before, 0.0)
    around = after + before
    after = 2.0 * after
    for y in range(ny):
        applied_ref[y * nz : (y + 1) * nz, :] = (
            around[:, y : y + 1] * own_ref[y] - after[:, y : y + 1] * halo_ref[y]
        )
    parts = laid(split(applied_ref[...], 3), THREE, 1, 0)
    parts_ref[...] = parts
    half = width // 2
    first = place_ref[0] == 0
    cross = gram_ref[width:, :] + jnp.dot(
        turned_ref[width:, :], parts, preferred_element_type=jnp.float32
    )
    cross = 0.5 * jnp.where(first, cross.T, cross)
    cross_ref[...] = jnp.where(first, cross[:half], cross[half:])
    sent_ref[...] = jnp.where(first, cross[half:], cross[:half])


def own_kernel(gram_ref, turned_ref, parts_ref, packed_ref):
    width = parts_ref.shape[1]
    half = width // 2
    own = gram_ref[:width, :] + jnp.dot(
        turned_ref[:width, :], parts_ref[...], preferred_element_type=jnp.float32
    )
    own = 0.5 * (own + own.T)
    row = lax.broadcasted_iota(jnp.int32, (half, width), 0)
    col = lax.broadcasted_iota(jnp.int32, (half, width), 1)
    packed_ref[:half, :] = jnp.where(col >= row, own[:half], pltpu.roll(own[half:], half, 1))
    packed_ref[half:, :] = column_sums(
        jnp.where(
            lax.broadcasted_iota(jnp.int32, (width, width), 0)
            == lax.broadcasted_iota(jnp.int32, (width, width), 1),
            own,
            0.0,
        )
    )


def unpacked(share):
    n = share.shape[1]
    h = n // 2
    top = share[:h]
    row = lax.broadcasted_iota(jnp.int32, (h, n), 0)
    col = lax.broadcasted_iota(jnp.int32, (h, n), 1)
    mirror = top.T
    wide = jnp.concatenate([mirror[:h], mirror[:h]], axis=1)
    first = jnp.where(col >= row, top, wide)
    second = jnp.where(col - h < row, pltpu.roll(top, h, 1), wide)
    second = jnp.where(col - h == row, share[h : h + 1], second)
    tall = jnp.concatenate([mirror[h:], mirror[h:]], axis=1)
    return jnp.concatenate([first, jnp.where(col < h, tall, second)], axis=0)


def rotation(diagonal, opposite, coupling, first):
    g_first = jnp.where(first, diagonal, opposite)
    g_second = jnp.where(first, opposite, diagonal)
    spread = g_first - g_second
    radius = jnp.sqrt(spread * spread + 4.0 * coupling * coupling)
    turned = jnp.where(spread > 0, -2.0, jnp.where(spread < 0, 2.0, 0.0)) * coupling
    tangent = turned * pl.reciprocal(
        jnp.abs(spread) + radius + 1e-06 * (g_first + g_second + 1.0), approx=False
    )
    cosine = lax.rsqrt(1.0 + tangent * tangent)
    sine = cosine * tangent
    return cosine, jnp.where(first, -sine, sine)


def tournament_kernel(
    meets, turns, place_ref, mine_ref, theirs_ref, code_ref, own_ref, other_ref, rotated_ref, sigma_ref
):
    n = own_ref.shape[2]
    h = n // 2
    side = place_ref[0] == 0
    mine, theirs = mine_ref[...], theirs_ref[...]
    zero_side = jnp.where(side, mine, theirs)
    one_side = jnp.where(side, theirs, mine)
    eye = lax.broadcasted_iota(jnp.int32, (n, n), 0) == lax.broadcasted_iota(jnp.int32, (n, n), 1)
    blank = jnp.zeros((n, n), jnp.float32)
    low_half = lax.broadcasted_iota(jnp.int32, (h, n), 1) < h
    low = lax.broadcasted_iota(jnp.int32, (2 * n, n), 1) < h

    tiles = range(n // 8)
    rows = [lax.broadcasted_iota(jnp.int32, (8, n), 0) + 8 * i for i in tiles]
    cols = lax.broadcasted_iota(jnp.int32, (8, n), 1)
    near = [unpacked(zero_side), unpacked(one_side)]
    cross = jnp.concatenate([zero_side[h + 8 :], one_side[h + 8 :]], axis=0)
    diagonal = [column_sums(jnp.where(eye, near[d], 0.0)) for d in range(2)]
    total = None
    slots = [[0, 1], [2, 3]]
    upper, lower = [0, 2], [1, 3]
    for meeting in range(meets):
        last = meeting == meets - 1
        uppers = {frozenset((upper[d], lower[d])): upper[d] for d in range(2)}
        swapped = [uppers[frozenset(slots[d])] != slots[d][0] for d in range(2)]
        factor = [None, None]
        near = [[near[d][8 * i : 8 * i + 8] for i in tiles] for d in range(2)]
        cross = [cross[8 * i : 8 * i + 8] for i in tiles]
        for turn in range(turns):
            index = meeting * turns + turn
            told = jnp.broadcast_to(code_ref[index : index + 1, :], (8, n))
            other_way = pltpu.roll(told, h, 1)
            for d in range(2):
                partner = (other_way % n) ^ h if swapped[d] else told % n
                first = (other_way if swapped[d] else told) >= n
                if turn == 0:
                    coupling = [
                        jnp.where(rows[i] == partner, near[d][i], 0.0) for i in tiles
                    ]
                else:
                    opposite = [lanes(part, partner) for part in factor[d]]
                    coupling = [left * right for left, right in zip(opposite, near[d])]
                while len(coupling) > 1:
                    coupling = [a + b for a, b in zip(coupling[::2], coupling[1::2])]
                coupling = column_sums(coupling[0])
                across = lanes(diagonal[d], partner)
                cosine, sine = rotation(diagonal[d], across, coupling, first)
                diagonal[d] = (
                    cosine * cosine * diagonal[d] + 2.0 * cosine * sine * coupling + sine * sine * across
                )
                if turn == 0:
                    factor[d] = [
                        jnp.where(rows[i] == cols, cosine, jnp.where(rows[i] == partner, sine, 0.0))
                        for i in tiles
                    ]
                else:
                    factor[d] = [
                        part * cosine + away * sine for part, away in zip(factor[d], opposite)
                    ]
                if not last or turn < turns - 1:
                    near[d] = [part * cosine + lanes(part, partner) * sine for part in near[d]]
                if not last and d == 1:
                    cross = [part * cosine + lanes(part, partner) * sine for part in cross]
        factor = [jnp.concatenate(factor[d], axis=0) for d in range(2)]
        if last:
            break
        near = [jnp.concatenate(near[d], axis=0) for d in range(2)]
        cross = jnp.concatenate(cross, axis=0)
        top = long_dot(factor[0].T, jnp.concatenate([near[0], cross], axis=1), THREE)
        g00, g01 = top[:, :n], top[:, n:]
        g11 = long_dot(factor[1].T, near[1], THREE)
        g10 = g01.T
        upper, lower = [upper[0], lower[0]], [lower[1], upper[1]]
        meets_next = [frozenset((upper[d], lower[d])) for d in range(2)]
        rolled = frozenset((slots[0][0], slots[1][1])) not in meets_next
        if rolled:
            slots[1] = slots[1][::-1]
            g01, g11 = pltpu.roll(g01, h, 1), pltpu.roll(g11, h, 1)
            g10 = jnp.concatenate([g10[h:], g10[:h]], axis=0)
            g11 = jnp.concatenate([g11[h:], g11[:h]], axis=0)
            diagonal[1] = pltpu.roll(diagonal[1], h, 1)
        slots = [[slots[0][0], slots[1][1]], [slots[1][0], slots[0][1]]]

        def mixed(first, second, third, fourth):
            return jnp.concatenate(
                [
                    jnp.where(low_half, first[:h], second[:h]),
                    jnp.where(low_half, third[h:], fourth[h:]),
                ],
                axis=0,
            )

        near = [mixed(g00, g01, g10, g11), mixed(g11, g10, g01, g00)]
        cross = mixed(g01, g00, g11, g10)
        diagonal = [
            jnp.where(cols < h, diagonal[0], diagonal[1]),
            jnp.where(cols < h, diagonal[1], diagonal[0]),
        ]
        if total is None:
            total = [
                jnp.concatenate([factor[0], blank], axis=0),
                jnp.concatenate([blank, factor[1]], axis=0),
            ]
        else:
            total = [long_dot(total[d], factor[d], TWO) for d in range(2)]
        if rolled:
            total[1] = pltpu.roll(total[1], h, 1)
        total = [jnp.where(low, total[0], total[1]), jnp.where(low, total[1], total[0])]

    flat = jnp.concatenate(
        [own_ref[...].reshape(-1, n), other_ref[...].reshape(-1, n)], axis=1
    )
    both = jnp.concatenate(total, axis=1)
    both = jnp.concatenate(
        [jnp.where(side, both[:n], both[n:]), jnp.where(side, both[n:], both[:n])], axis=0
    )
    before_last = long_dot(flat, both, TWO)
    gap = jnp.zeros((n, h), jnp.float32)
    blocks, norms = {}, {}
    for d in range(2):
        norm = jnp.sqrt(diagonal[d][:1])
        for i in range(2):
            part = factor[d][:, i * h : (i + 1) * h]
            blocks[slots[d][i]] = jnp.concatenate([part, gap] if d == 0 else [gap, part], axis=0)
            norms[slots[d][i]] = norm[:, i * h : (i + 1) * h]
    picked = jnp.where(
        side,
        jnp.concatenate([blocks[0], blocks[1]], axis=1),
        jnp.concatenate([blocks[2], blocks[3]], axis=1),
    )
    rotated_ref[...] = long_dot(before_last, picked, TWO).reshape(rotated_ref.shape)
    sigma_ref[...] = jnp.where(
        side,
        jnp.concatenate([norms[0], norms[1]], axis=1),
        jnp.concatenate([norms[2], norms[3]], axis=1),
    )


def shards(snapshots, labels, conductivity, pairing):
    planes, ny, nz, width = snapshots.shape
    cells = planes * ny * nz
    half = width // 2
    count = lax.axis_size("rows")
    swap = [(0, 1), (1, 0)]
    own = snapshots[0]
    labels = labels[0].T
    halo = lax.ppermute(own, "rows", [(i + 2, i) for i in range(count - 2)])
    other = lax.ppermute(own, "cols", swap)
    place = jnp.stack(
        [lax.axis_index("cols"), lax.axis_index("rows"), jnp.asarray(count, jnp.int32)]
    ).astype(jnp.int32)

    code = pl.pallas_call(
        code_kernel,
        out_shape=jax.ShapeDtypeStruct((pairing.shape[0] * pairing.shape[1], width), jnp.int32),
        in_specs=[VMEM],
        out_specs=VMEM,
        compiler_params=PARAMS,
    )(pairing)
    beside = lax.ppermute(
        labels,
        ("rows", "cols"),
        [(2 * i, 2 * (i ^ 1)) for i in range(count)]
        + [(2 * i + 1, 2 * (i + (1 if i % 2 else -1)) + 1) for i in range(1, count - 1)],
    )
    gram, turned, own, table = pl.pallas_call(
        local_kernel,
        out_shape=(
            jax.ShapeDtypeStruct((2 * width, width), jnp.float32),
            jax.ShapeDtypeStruct((2 * width, len(THREE) * cells), jnp.bfloat16),
            jax.ShapeDtypeStruct((ny, nz, width), jnp.float32),
            jax.ShapeDtypeStruct((conductivity.shape[0], width), jnp.float32),
        ),
        in_specs=[HBM] * 3 + [VMEM],
        out_specs=[VMEM] * 4,
        scratch_shapes=[
            pltpu.VMEM((cells, width), jnp.float32),
            pltpu.VMEM(labels.shape, jnp.int32),
            pltpu.SMEM(conductivity.shape, jnp.float32),
            pltpu.SemaphoreType.DMA((3,)),
        ],
        compiler_params=PARAMS,
    )(*[pltpu.with_memory_space_constraint(value, pltpu.HBM) for value in (conductivity, own, labels)], other)
    beside, table = lax.optimization_barrier((beside, table))
    across = lax.ppermute(beside, "cols", swap)
    parts, cross, sent = pl.pallas_call(
        halo_kernel,
        out_shape=(
            jax.ShapeDtypeStruct((len(THREE) * cells, width), jnp.bfloat16),
            jax.ShapeDtypeStruct((half, width), jnp.float32),
            jax.ShapeDtypeStruct((half, width), jnp.float32),
        ),
        in_specs=[SMEM] + [VMEM] * 7,
        out_specs=[VMEM] * 3,
        scratch_shapes=[pltpu.VMEM((cells, width), jnp.float32)],
        compiler_params=PARAMS,
    )(place, table, own, halo, beside, across, gram, turned)
    received = lax.ppermute(sent, "cols", swap)
    packed = pl.pallas_call(
        own_kernel,
        out_shape=jax.ShapeDtypeStruct((half + 8, width), jnp.float32),
        in_specs=[VMEM] * 3,
        out_specs=VMEM,
        compiler_params=PARAMS,
    )(gram, turned, parts)
    share = jnp.concatenate([packed, cross + received], axis=0)
    apart = 1
    while apart < count:
        share = share + lax.ppermute(share, "rows", [(i, i ^ apart) for i in range(count)])
        apart *= 2
    theirs = lax.ppermute(share, "cols", swap)
    rotated, sigma = pl.pallas_call(
        functools.partial(tournament_kernel, pairing.shape[0], pairing.shape[1]),
        out_shape=(
            jax.ShapeDtypeStruct((ny, nz, width), jnp.float32),
            jax.ShapeDtypeStruct((1, width), jnp.float32),
        ),
        in_specs=[SMEM] + [VMEM] * 5,
        out_specs=[VMEM] * 2,
        compiler_params=PARAMS,
    )(place, share, theirs, code, own, other)
    return rotated.reshape(snapshots.shape), sigma.reshape(width)


def solution(mesh):
    placed = (
        P(("groups", "rows"), None, None, "cols"),
        P(("groups", "rows"), None, None),
        P("groups"),
        P(),
    )
    return jax.shard_map(
        shards,
        mesh=mesh,
        in_specs=placed,
        out_specs=(P(("groups", "rows"), None, None, "cols"), P(("groups", "cols"))),
        check_vma=False,
    )
```

```python
import functools

import jax
import jax.numpy as jnp
from jax import lax
from jax.experimental import pallas as pl
from jax.experimental.pallas import tpu as pltpu
from jax.sharding import PartitionSpec as P

PARAMS = pltpu.CompilerParams(vmem_limit_bytes=16 * 2**20)
HBM = pl.BlockSpec(memory_space=pltpu.HBM)
VMEM = pl.BlockSpec(memory_space=pltpu.VMEM)
SMEM = pl.BlockSpec(memory_space=pltpu.SMEM)


def lanes(values, index):
    return jnp.take_along_axis(
        values, jnp.broadcast_to(index, values.shape), axis=1, mode="promise_in_bounds"
    )


def code_kernel(pairing_ref, code_ref):
    meets, turns, n = pairing_ref.shape
    pairs = jnp.concatenate([pairing_ref[m] for m in range(meets)], axis=0)
    place = lax.broadcasted_iota(jnp.int32, pairs.shape, 1)
    told = lanes(pairs, place ^ 1) + jnp.where(place % 2 == 0, n, 0)
    pairs = pairs.astype(jnp.float32).T
    told = told.astype(jnp.float32).T
    col = lax.broadcasted_iota(jnp.int32, (n, n), 1).astype(jnp.float32)
    rows = []
    for index in range(meets * turns):
        here = pairs[:, index : index + 1] == col
        rows.append(jnp.sum(jnp.where(here, told[:, index : index + 1], 0.0), axis=0, keepdims=True))
    code_ref[...] = jnp.concatenate(rows, axis=0).astype(jnp.int32)


def split(values, count):
    parts = []
    for index in range(count):
        part = values.astype(jnp.bfloat16)
        parts.append(part)
        if index < count - 1:
            values = values - part.astype(jnp.float32)
    return parts


TWO = ((0, 0), (0, 1), (1, 0))
THREE = TWO + ((0, 2), (1, 1), (2, 0))


def long_dot(left, right, terms):
    count = 1 + max(i for i, _ in terms)
    left, right = split(left, count), split(right, count)
    return jnp.dot(
        laid(left, terms, 0, 1), laid(right, terms, 1, 0), preferred_element_type=jnp.float32
    )


def laid(parts, terms, side, axis):
    return jnp.concatenate([parts[term[side]] for term in terms], axis=axis)


def column_sums(values):
    return jnp.broadcast_to(jnp.sum(values, axis=0, keepdims=True), (8, values.shape[1]))


def quarter_squares(labels, table):
    squares = jnp.zeros(labels.shape, jnp.float32)
    for region in range(table.shape[0]):
        squares = jnp.where(labels == region, table[region : region + 1, : labels.shape[1]], squares)
    return squares


def local_kernel(
    conductivity_ref, own_hbm_ref, labels_hbm_ref, other_ref,
    gram_ref, turned_ref, own_ref, table_ref,
    applied_ref, labels_ref, regions_ref, sems,
):
    ny, nz, width = own_ref.shape
    cells = ny * nz
    fetches = [
        pltpu.make_async_copy(source, target, sems.at[index])
        for index, (source, target) in enumerate(
            ((own_hbm_ref, own_ref), (labels_hbm_ref, labels_ref), (conductivity_ref, regions_ref))
        )
    ]
    for fetch in fetches:
        fetch.start()
    turned_ref[width:, :] = laid(split(other_ref[...].reshape(cells, width).T, 3), THREE, 0, 1)
    for fetch in fetches:
        fetch.wait()
    table_ref[...] = jnp.concatenate(
        [jnp.full((1, width), 0.25 * regions_ref[region]) for region in range(table_ref.shape[0])],
        axis=0,
    )
    squares = quarter_squares(labels_ref[...], table_ref[...])
    z = lax.broadcasted_iota(jnp.int32, (nz, ny), 0)
    above = jnp.where(z < nz - 1, pltpu.roll(squares, nz - 1, 0), 0.0)
    below = jnp.where(z > 0, pltpu.roll(squares, 1, 0), 0.0)
    inner = 1.0 + above + below
    above = jnp.where(z < nz - 2, above, 0.0)
    below = jnp.where(z > 1, below, 0.0)
    for y in range(ny):
        u = own_ref[y]
        scale = inner[:, y : y + 1]
        if y > 0:
            scale += squares[:, y - 1 : y]
        if y < ny - 1:
            scale += squares[:, y + 1 : y + 2]
        total = scale * u
        if y > 1:
            total -= squares[:, y - 1 : y] * own_ref[y - 2]
        if y < ny - 2:
            total -= squares[:, y + 1 : y + 2] * own_ref[y + 2]
        total -= above[:, y : y + 1] * pltpu.roll(u, nz - 2, 0)
        total -= below[:, y : y + 1] * pltpu.roll(u, 2, 0)
        applied_ref[y * nz : (y + 1) * nz, :] = total
    turned_ref[:width, :] = laid(split(own_ref[...].reshape(cells, width).T, 3), THREE, 0, 1)
    gram_ref[...] = jnp.dot(
        turned_ref[...],
        laid(split(applied_ref[...], 3), THREE, 1, 0),
        preferred_element_type=jnp.float32,
    )


def halo_kernel(
    count, table_ref, own_ref, halo_ref, mine_ref, theirs_ref, gram_ref, turned_ref,
    applied_ref, cross_ref, sent_ref,
):
    ny, nz, width = own_ref.shape
    mine = quarter_squares(mine_ref[...], table_ref[...])
    theirs = quarter_squares(theirs_ref[...], table_ref[...])
    row = lax.axis_index("rows")
    ahead_first = lax.axis_index("cols") == row % 2
    after = jnp.where(ahead_first, mine, theirs)
    before = jnp.where(ahead_first, theirs, mine)
    after = jnp.where(row < count - 1, after, 0.0)
    before = jnp.where(row > 0, before, 0.0)
    around = after + before
    after = 2.0 * after
    for y in range(ny):
        applied_ref[y * nz : (y + 1) * nz, :] = (
            around[:, y : y + 1] * own_ref[y] - after[:, y : y + 1] * halo_ref[y]
        )
    parts = laid(split(applied_ref[...], 3), THREE, 1, 0)
    half = width // 2
    first = lax.axis_index("cols") == 0
    cross = gram_ref[width:, :] + jnp.dot(
        turned_ref[width:, :], parts, preferred_element_type=jnp.float32
    )
    cross = 0.5 * jnp.where(first, cross.T, cross)
    cross_ref[...] = jnp.where(first, cross[:half], cross[half:])
    sent_ref[...] = jnp.where(first, cross[half:], cross[:half])


def own_kernel(gram_ref, turned_ref, applied_ref, packed_ref):
    width = applied_ref.shape[1]
    half = width // 2
    own = gram_ref[:width, :] + jnp.dot(
        turned_ref[:width, :],
        laid(split(applied_ref[...], 3), THREE, 1, 0),
        preferred_element_type=jnp.float32,
    )
    own = 0.5 * (own + own.T)
    row = lax.broadcasted_iota(jnp.int32, (half, width), 0)
    col = lax.broadcasted_iota(jnp.int32, (half, width), 1)
    packed_ref[:half, :] = jnp.where(col >= row, own[:half], pltpu.roll(own[half:], half, 1))
    packed_ref[half:, :] = column_sums(
        jnp.where(
            lax.broadcasted_iota(jnp.int32, (width, width), 0)
            == lax.broadcasted_iota(jnp.int32, (width, width), 1),
            own,
            0.0,
        )
    )


def unpacked(share):
    n = share.shape[1]
    h = n // 2
    top = share[:h]
    row = lax.broadcasted_iota(jnp.int32, (h, n), 0)
    col = lax.broadcasted_iota(jnp.int32, (h, n), 1)
    mirror = top.T
    wide = jnp.concatenate([mirror[:h], mirror[:h]], axis=1)
    first = jnp.where(col >= row, top, wide)
    second = jnp.where(col - h < row, pltpu.roll(top, h, 1), wide)
    second = jnp.where(col - h == row, share[h : h + 1], second)
    tall = jnp.concatenate([mirror[h:], mirror[h:]], axis=1)
    return jnp.concatenate([first, jnp.where(col < h, tall, second)], axis=0)


def rotation(diagonal, opposite, coupling, first):
    g_first = jnp.where(first, diagonal, opposite)
    g_second = jnp.where(first, opposite, diagonal)
    spread = g_first - g_second
    radius = jnp.sqrt(spread * spread + 4.0 * coupling * coupling)
    turned = jnp.where(spread > 0, -2.0, jnp.where(spread < 0, 2.0, 0.0)) * coupling
    tangent = turned * pl.reciprocal(
        jnp.abs(spread) + radius + 1e-06 * (g_first + g_second + 1.0), approx=False
    )
    cosine = lax.rsqrt(1.0 + tangent * tangent)
    sine = cosine * tangent
    return cosine, jnp.where(first, -sine, sine)


def tournament_kernel(
    meets, turns, mine_ref, theirs_ref, code_ref, own_ref, other_ref, rotated_ref, sigma_ref
):
    n = own_ref.shape[2]
    h = n // 2
    side = lax.axis_index("cols") == 0
    mine, theirs = mine_ref[...], theirs_ref[...]
    zero_side = jnp.where(side, mine, theirs)
    one_side = jnp.where(side, theirs, mine)
    eye = lax.broadcasted_iota(jnp.int32, (n, n), 0) == lax.broadcasted_iota(jnp.int32, (n, n), 1)
    blank = jnp.zeros((n, n), jnp.float32)
    low_half = lax.broadcasted_iota(jnp.int32, (h, n), 1) < h
    low = lax.broadcasted_iota(jnp.int32, (2 * n, n), 1) < h

    tiles = range(n // 8)
    rows = [lax.broadcasted_iota(jnp.int32, (8, n), 0) + 8 * i for i in tiles]
    cols = lax.broadcasted_iota(jnp.int32, (8, n), 1)
    near = [unpacked(zero_side), unpacked(one_side)]
    cross = jnp.concatenate([zero_side[h + 8 :], one_side[h + 8 :]], axis=0)
    diagonal = [column_sums(jnp.where(eye, near[d], 0.0)) for d in range(2)]
    total = None
    slots = [[0, 1], [2, 3]]
    upper, lower = [0, 2], [1, 3]
    for meeting in range(meets):
        last = meeting == meets - 1
        uppers = {frozenset((upper[d], lower[d])): upper[d] for d in range(2)}
        swapped = [uppers[frozenset(slots[d])] != slots[d][0] for d in range(2)]
        factor = [None, None]
        near = [[near[d][8 * i : 8 * i + 8] for i in tiles] for d in range(2)]
        cross = [cross[8 * i : 8 * i + 8] for i in tiles]
        for turn in range(turns):
            index = meeting * turns + turn
            told = jnp.broadcast_to(code_ref[index : index + 1, :], (8, n))
            other_way = pltpu.roll(told, h, 1)
            for d in range(2):
                partner = (other_way % n) ^ h if swapped[d] else told % n
                first = (other_way if swapped[d] else told) >= n
                if turn == 0:
                    coupling = [
                        jnp.where(rows[i] == partner, near[d][i], 0.0) for i in tiles
                    ]
                else:
                    opposite = [lanes(part, partner) for part in factor[d]]
                    coupling = [left * right for left, right in zip(opposite, near[d])]
                while len(coupling) > 1:
                    coupling = [a + b for a, b in zip(coupling[::2], coupling[1::2])]
                coupling = column_sums(coupling[0])
                across = lanes(diagonal[d], partner)
                cosine, sine = rotation(diagonal[d], across, coupling, first)
                diagonal[d] = (
                    cosine * cosine * diagonal[d] + 2.0 * cosine * sine * coupling + sine * sine * across
                )
                if turn == 0:
                    factor[d] = [
                        jnp.where(rows[i] == cols, cosine, jnp.where(rows[i] == partner, sine, 0.0))
                        for i in tiles
                    ]
                else:
                    factor[d] = [
                        part * cosine + away * sine for part, away in zip(factor[d], opposite)
                    ]
                if not last or turn < turns - 1:
                    near[d] = [part * cosine + lanes(part, partner) * sine for part in near[d]]
                if not last and d == 1:
                    cross = [part * cosine + lanes(part, partner) * sine for part in cross]
        factor = [jnp.concatenate(factor[d], axis=0) for d in range(2)]
        if last:
            break
        near = [jnp.concatenate(near[d], axis=0) for d in range(2)]
        cross = jnp.concatenate(cross, axis=0)
        top = long_dot(factor[0].T, jnp.concatenate([near[0], cross], axis=1), THREE)
        g00, g01 = top[:, :n], top[:, n:]
        g11 = long_dot(factor[1].T, near[1], THREE)
        g10 = g01.T
        upper, lower = [upper[0], lower[0]], [lower[1], upper[1]]
        meets_next = [frozenset((upper[d], lower[d])) for d in range(2)]
        rolled = frozenset((slots[0][0], slots[1][1])) not in meets_next
        if rolled:
            slots[1] = slots[1][::-1]
            g01, g11 = pltpu.roll(g01, h, 1), pltpu.roll(g11, h, 1)
            g10 = jnp.concatenate([g10[h:], g10[:h]], axis=0)
            g11 = jnp.concatenate([g11[h:], g11[:h]], axis=0)
            diagonal[1] = pltpu.roll(diagonal[1], h, 1)
        slots = [[slots[0][0], slots[1][1]], [slots[1][0], slots[0][1]]]

        def mixed(first, second, third, fourth):
            return jnp.concatenate(
                [
                    jnp.where(low_half, first[:h], second[:h]),
                    jnp.where(low_half, third[h:], fourth[h:]),
                ],
                axis=0,
            )

        near = [mixed(g00, g01, g10, g11), mixed(g11, g10, g01, g00)]
        cross = mixed(g01, g00, g11, g10)
        diagonal = [
            jnp.where(cols < h, diagonal[0], diagonal[1]),
            jnp.where(cols < h, diagonal[1], diagonal[0]),
        ]
        if total is None:
            total = [
                jnp.concatenate([factor[0], blank], axis=0),
                jnp.concatenate([blank, factor[1]], axis=0),
            ]
        else:
            total = [long_dot(total[d], factor[d], TWO) for d in range(2)]
        if rolled:
            total[1] = pltpu.roll(total[1], h, 1)
        total = [jnp.where(low, total[0], total[1]), jnp.where(low, total[1], total[0])]

    flat = jnp.concatenate(
        [own_ref[...].reshape(-1, n), other_ref[...].reshape(-1, n)], axis=1
    )
    both = jnp.concatenate(total, axis=1)
    both = jnp.concatenate(
        [jnp.where(side, both[:n], both[n:]), jnp.where(side, both[n:], both[:n])], axis=0
    )
    before_last = long_dot(flat, both, TWO)
    gap = jnp.zeros((n, h), jnp.float32)
    blocks, norms = {}, {}
    for d in range(2):
        norm = jnp.sqrt(diagonal[d][:1])
        for i in range(2):
            part = factor[d][:, i * h : (i + 1) * h]
            blocks[slots[d][i]] = jnp.concatenate([part, gap] if d == 0 else [gap, part], axis=0)
            norms[slots[d][i]] = norm[:, i * h : (i + 1) * h]
    picked = jnp.where(
        side,
        jnp.concatenate([blocks[0], blocks[1]], axis=1),
        jnp.concatenate([blocks[2], blocks[3]], axis=1),
    )
    rotated_ref[...] = long_dot(before_last, picked, TWO).reshape(rotated_ref.shape)
    sigma_ref[...] = jnp.where(
        side,
        jnp.concatenate([norms[0], norms[1]], axis=1),
        jnp.concatenate([norms[2], norms[3]], axis=1),
    )


def shards(snapshots, labels, conductivity, pairing):
    planes, ny, nz, width = snapshots.shape
    cells = planes * ny * nz
    half = width // 2
    count = lax.axis_size("rows")
    swap = [(0, 1), (1, 0)]
    own = snapshots[0]
    labels = labels[0].T
    halo = lax.ppermute(own, "rows", [(i + 2, i) for i in range(count - 2)])
    other = lax.ppermute(own, "cols", swap)
    code = pl.pallas_call(
        code_kernel,
        out_shape=jax.ShapeDtypeStruct((pairing.shape[0] * pairing.shape[1], width), jnp.int32),
        in_specs=[VMEM],
        out_specs=VMEM,
        compiler_params=PARAMS,
    )(pairing)
    beside = lax.ppermute(
        labels,
        ("rows", "cols"),
        [(2 * i, 2 * (i ^ 1)) for i in range(count)]
        + [(2 * i + 1, 2 * (i + (1 if i % 2 else -1)) + 1) for i in range(1, count - 1)],
    )
    gram, turned, own, table = pl.pallas_call(
        local_kernel,
        out_shape=(
            jax.ShapeDtypeStruct((2 * width, width), jnp.float32),
            jax.ShapeDtypeStruct((2 * width, len(THREE) * cells), jnp.bfloat16),
            jax.ShapeDtypeStruct((ny, nz, width), jnp.float32),
            jax.ShapeDtypeStruct((conductivity.shape[0], width), jnp.float32),
        ),
        in_specs=[HBM] * 3 + [VMEM],
        out_specs=[VMEM] * 4,
        scratch_shapes=[
            pltpu.VMEM((cells, width), jnp.float32),
            pltpu.VMEM(labels.shape, jnp.int32),
            pltpu.SMEM(conductivity.shape, jnp.float32),
            pltpu.SemaphoreType.DMA((3,)),
        ],
        compiler_params=PARAMS,
    )(*[pltpu.with_memory_space_constraint(value, pltpu.HBM) for value in (conductivity, own, labels)], other)
    beside, table = lax.optimization_barrier((beside, table))
    across = lax.ppermute(beside, "cols", swap)
    applied, cross, sent = pl.pallas_call(
        functools.partial(halo_kernel, count),
        out_shape=(
            jax.ShapeDtypeStruct((cells, width), jnp.float32),
            jax.ShapeDtypeStruct((half, width), jnp.float32),
            jax.ShapeDtypeStruct((half, width), jnp.float32),
        ),
        in_specs=[VMEM] * 7,
        out_specs=[VMEM] * 3,
        compiler_params=PARAMS,
    )(table, own, halo, beside, across, gram, turned)
    received = lax.ppermute(sent, "cols", swap)
    packed = pl.pallas_call(
        own_kernel,
        out_shape=jax.ShapeDtypeStruct((half + 8, width), jnp.float32),
        in_specs=[VMEM] * 3,
        out_specs=VMEM,
        compiler_params=PARAMS,
    )(gram, turned, applied)
    share = jnp.concatenate([packed, cross + received], axis=0)
    apart = 1
    while apart < count:
        share = share + lax.ppermute(share, "rows", [(i, i ^ apart) for i in range(count)])
        apart *= 2
    theirs = lax.ppermute(share, "cols", swap)
    rotated, sigma = pl.pallas_call(
        functools.partial(tournament_kernel, pairing.shape[0], pairing.shape[1]),
        out_shape=(
            jax.ShapeDtypeStruct((ny, nz, width), jnp.float32),
            jax.ShapeDtypeStruct((1, width), jnp.float32),
        ),
        in_specs=[VMEM] * 5,
        out_specs=[VMEM] * 2,
        compiler_params=PARAMS,
    )(share, theirs, code, own, other)
    return rotated.reshape(snapshots.shape), sigma.reshape(width)


def solution(mesh):
    placed = (
        P(("groups", "rows"), None, None, "cols"),
        P(("groups", "rows"), None, None),
        P("groups"),
        P(),
    )
    return jax.shard_map(
        shards,
        mesh=mesh,
        in_specs=placed,
        out_specs=(P(("groups", "rows"), None, None, "cols"), P(("groups", "cols"))),
        check_vma=False,
    )
```

```python
import functools

import jax
import jax.numpy as jnp
from jax import lax
from jax.experimental import pallas as pl
from jax.experimental.pallas import tpu as pltpu
from jax.sharding import PartitionSpec as P

PARAMS = pltpu.CompilerParams(vmem_limit_bytes=16 * 2**20)
HBM = pl.BlockSpec(memory_space=pltpu.HBM)
VMEM = pl.BlockSpec(memory_space=pltpu.VMEM)
SMEM = pl.BlockSpec(memory_space=pltpu.SMEM)


def lanes(values, index):
    return jnp.take_along_axis(
        values, jnp.broadcast_to(index, values.shape), axis=1, mode="promise_in_bounds"
    )


def code_kernel(pairing_ref, code_ref):
    meets, turns, n = pairing_ref.shape
    pairs = jnp.concatenate([pairing_ref[m] for m in range(meets)], axis=0)
    place = lax.broadcasted_iota(jnp.int32, pairs.shape, 1)
    told = lanes(pairs, place ^ 1) + jnp.where(place % 2 == 0, n, 0)
    pairs = pairs.astype(jnp.float32).T
    told = told.astype(jnp.float32).T
    col = lax.broadcasted_iota(jnp.int32, (n, n), 1).astype(jnp.float32)
    rows = []
    for index in range(meets * turns):
        here = pairs[:, index : index + 1] == col
        rows.append(jnp.sum(jnp.where(here, told[:, index : index + 1], 0.0), axis=0, keepdims=True))
    code_ref[...] = jnp.concatenate(rows, axis=0).astype(jnp.int32)


def split(values, count):
    parts = []
    for index in range(count):
        part = values.astype(jnp.bfloat16)
        parts.append(part)
        if index < count - 1:
            values = values - part.astype(jnp.float32)
    return parts


TWO = ((0, 0), (0, 1), (1, 0))
THREE = TWO + ((0, 2), (1, 1), (2, 0))


def long_dot(left, right, terms):
    count = 1 + max(i for i, _ in terms)
    left, right = split(left, count), split(right, count)
    return jnp.dot(
        laid(left, terms, 0, 1), laid(right, terms, 1, 0), preferred_element_type=jnp.float32
    )


def laid(parts, terms, side, axis):
    return jnp.concatenate([parts[term[side]] for term in terms], axis=axis)


def column_sums(values):
    return jnp.broadcast_to(jnp.sum(values, axis=0, keepdims=True), (8, values.shape[1]))


def quarter_squares(labels, table):
    squares = jnp.zeros(labels.shape, jnp.float32)
    for region in range(table.shape[0]):
        squares = jnp.where(labels == region, table[region : region + 1, : labels.shape[1]], squares)
    return squares


def local_kernel(
    conductivity_ref, own_hbm_ref, labels_hbm_ref, other_ref,
    gram_ref, turned_ref, own_ref, table_ref,
    applied_ref, labels_ref, regions_ref, sems,
):
    ny, nz, width = own_ref.shape
    cells = ny * nz
    fetches = [
        pltpu.make_async_copy(source, target, sems.at[index])
        for index, (source, target) in enumerate(
            ((own_hbm_ref, own_ref), (labels_hbm_ref, labels_ref), (conductivity_ref, regions_ref))
        )
    ]
    for fetch in fetches:
        fetch.start()
    turned_ref[width:, :] = laid(split(other_ref[...].reshape(cells, width).T, 3), THREE, 0, 1)
    for fetch in fetches:
        fetch.wait()
    table_ref[...] = jnp.concatenate(
        [jnp.full((1, width), 0.25 * regions_ref[region]) for region in range(table_ref.shape[0])],
        axis=0,
    )
    squares = quarter_squares(labels_ref[...], table_ref[...])
    z = lax.broadcasted_iota(jnp.int32, (nz, ny), 0)
    above = jnp.where(z < nz - 1, pltpu.roll(squares, nz - 1, 0), 0.0)
    below = jnp.where(z > 0, pltpu.roll(squares, 1, 0), 0.0)
    inner = 1.0 + above + below
    above = jnp.where(z < nz - 2, above, 0.0)
    below = jnp.where(z > 1, below, 0.0)
    for y in range(ny):
        u = own_ref[y]
        scale = inner[:, y : y + 1]
        if y > 0:
            scale += squares[:, y - 1 : y]
        if y < ny - 1:
            scale += squares[:, y + 1 : y + 2]
        total = scale * u
        if y > 1:
            total -= squares[:, y - 1 : y] * own_ref[y - 2]
        if y < ny - 2:
            total -= squares[:, y + 1 : y + 2] * own_ref[y + 2]
        total -= above[:, y : y + 1] * pltpu.roll(u, nz - 2, 0)
        total -= below[:, y : y + 1] * pltpu.roll(u, 2, 0)
        applied_ref[y * nz : (y + 1) * nz, :] = total
    turned_ref[:width, :] = laid(split(own_ref[...].reshape(cells, width).T, 3), THREE, 0, 1)
    gram_ref[...] = jnp.dot(
        turned_ref[...],
        laid(split(applied_ref[...], 3), THREE, 1, 0),
        preferred_element_type=jnp.float32,
    )


def halo_kernel(
    count, table_ref, own_ref, halo_ref, mine_ref, theirs_ref, gram_ref, turned_ref,
    applied_ref, cross_ref, sent_ref,
):
    ny, nz, width = own_ref.shape
    mine = quarter_squares(mine_ref[...], table_ref[...])
    theirs = quarter_squares(theirs_ref[...], table_ref[...])
    row = lax.axis_index("rows")
    ahead_first = lax.axis_index("cols") == row % 2
    after = jnp.where(ahead_first, mine, theirs)
    before = jnp.where(ahead_first, theirs, mine)
    after = jnp.where(row < count - 1, after, 0.0)
    before = jnp.where(row > 0, before, 0.0)
    around = after + before
    after = 2.0 * after
    for y in range(ny):
        applied_ref[y * nz : (y + 1) * nz, :] = (
            around[:, y : y + 1] * own_ref[y] - after[:, y : y + 1] * halo_ref[y]
        )
    parts = laid(split(applied_ref[...], 3), THREE, 1, 0)
    half = width // 2
    first = lax.axis_index("cols") == 0
    cross = gram_ref[width:, :] + jnp.dot(
        turned_ref[width:, :], parts, preferred_element_type=jnp.float32
    )
    cross = 0.5 * jnp.where(first, cross.T, cross)
    cross_ref[...] = jnp.where(first, cross[:half], cross[half:])
    sent_ref[...] = jnp.where(first, cross[half:], cross[:half])


def own_kernel(gram_ref, turned_ref, applied_ref, packed_ref):
    width = applied_ref.shape[1]
    half = width // 2
    own = gram_ref[:width, :] + jnp.dot(
        turned_ref[:width, :],
        laid(split(applied_ref[...], 3), THREE, 1, 0),
        preferred_element_type=jnp.float32,
    )
    own = 0.5 * (own + own.T)
    row = lax.broadcasted_iota(jnp.int32, (half, width), 0)
    col = lax.broadcasted_iota(jnp.int32, (half, width), 1)
    packed_ref[:half, :] = jnp.where(col >= row, own[:half], pltpu.roll(own[half:], half, 1))
    packed_ref[half:, :] = column_sums(
        jnp.where(
            lax.broadcasted_iota(jnp.int32, (width, width), 0)
            == lax.broadcasted_iota(jnp.int32, (width, width), 1),
            own,
            0.0,
        )
    )


def unpacked(share):
    n = share.shape[1]
    h = n // 2
    top = share[:h]
    row = lax.broadcasted_iota(jnp.int32, (h, n), 0)
    col = lax.broadcasted_iota(jnp.int32, (h, n), 1)
    mirror = top.T
    wide = jnp.concatenate([mirror[:h], mirror[:h]], axis=1)
    first = jnp.where(col >= row, top, wide)
    second = jnp.where(col - h < row, pltpu.roll(top, h, 1), wide)
    second = jnp.where(col - h == row, share[h : h + 1], second)
    tall = jnp.concatenate([mirror[h:], mirror[h:]], axis=1)
    return jnp.concatenate([first, jnp.where(col < h, tall, second)], axis=0)


def rotation(diagonal, opposite, coupling, first):
    g_first = jnp.where(first, diagonal, opposite)
    g_second = jnp.where(first, opposite, diagonal)
    spread = g_first - g_second
    radius = jnp.sqrt(spread * spread + 4.0 * coupling * coupling)
    turned = jnp.where(spread > 0, -2.0, jnp.where(spread < 0, 2.0, 0.0)) * coupling
    tangent = turned * pl.reciprocal(
        jnp.abs(spread) + radius + 1e-06 * (g_first + g_second + 1.0), approx=False
    )
    cosine = lax.rsqrt(1.0 + tangent * tangent)
    sine = cosine * tangent
    return cosine, jnp.where(first, -sine, sine)


def tournament_kernel(
    meets, turns, mine_ref, theirs_ref, code_ref, own_ref, other_ref, rotated_ref, sigma_ref
):
    n = own_ref.shape[2]
    h = n // 2
    side = lax.axis_index("cols") == 0
    mine, theirs = mine_ref[...], theirs_ref[...]
    zero_side = jnp.where(side, mine, theirs)
    one_side = jnp.where(side, theirs, mine)
    eye = lax.broadcasted_iota(jnp.int32, (n, n), 0) == lax.broadcasted_iota(jnp.int32, (n, n), 1)
    blank = jnp.zeros((n, n), jnp.float32)
    low_half = lax.broadcasted_iota(jnp.int32, (h, n), 1) < h
    low = lax.broadcasted_iota(jnp.int32, (2 * n, n), 1) < h

    tiles = range(n // 8)
    rows = [lax.broadcasted_iota(jnp.int32, (8, n), 0) + 8 * i for i in tiles]
    cols = lax.broadcasted_iota(jnp.int32, (8, n), 1)
    near = [unpacked(zero_side), unpacked(one_side)]
    cross = jnp.concatenate([zero_side[h + 8 :], one_side[h + 8 :]], axis=0)
    diagonal = [column_sums(jnp.where(eye, near[d], 0.0)) for d in range(2)]
    total = None
    slots = [[0, 1], [2, 3]]
    upper, lower = [0, 2], [1, 3]
    for meeting in range(meets):
        last = meeting == meets - 1
        uppers = {frozenset((upper[d], lower[d])): upper[d] for d in range(2)}
        swapped = [uppers[frozenset(slots[d])] != slots[d][0] for d in range(2)]
        factor = [None, None]
        near = [[near[d][8 * i : 8 * i + 8] for i in tiles] for d in range(2)]
        cross = [cross[8 * i : 8 * i + 8] for i in tiles]
        for turn in range(turns):
            index = meeting * turns + turn
            told = jnp.broadcast_to(code_ref[index : index + 1, :], (8, n))
            other_way = pltpu.roll(told, h, 1)
            for d in range(2):
                partner = (other_way & (n - 1)) ^ h if swapped[d] else told & (n - 1)
                first = (other_way if swapped[d] else told) >= n
                if turn == 0:
                    coupling = [
                        jnp.where(rows[i] == partner, near[d][i], 0.0) for i in tiles
                    ]
                else:
                    opposite = [lanes(part, partner) for part in factor[d]]
                    coupling = [left * right for left, right in zip(opposite, near[d])]
                while len(coupling) > 1:
                    coupling = [a + b for a, b in zip(coupling[::2], coupling[1::2])]
                coupling = column_sums(coupling[0])
                across = lanes(diagonal[d], partner)
                cosine, sine = rotation(diagonal[d], across, coupling, first)
                diagonal[d] = (
                    cosine * cosine * diagonal[d] + 2.0 * cosine * sine * coupling + sine * sine * across
                )
                if turn == 0:
                    factor[d] = [
                        jnp.where(rows[i] == cols, cosine, jnp.where(rows[i] == partner, sine, 0.0))
                        for i in tiles
                    ]
                else:
                    factor[d] = [
                        part * cosine + away * sine for part, away in zip(factor[d], opposite)
                    ]
                if not last or turn < turns - 1:
                    near[d] = [part * cosine + lanes(part, partner) * sine for part in near[d]]
                if not last and d == 1:
                    cross = [part * cosine + lanes(part, partner) * sine for part in cross]
        factor = [jnp.concatenate(factor[d], axis=0) for d in range(2)]
        if last:
            break
        near = [jnp.concatenate(near[d], axis=0) for d in range(2)]
        cross = jnp.concatenate(cross, axis=0)
        top = long_dot(factor[0].T, jnp.concatenate([near[0], cross], axis=1), THREE)
        g00, g01 = top[:, :n], top[:, n:]
        g11 = long_dot(factor[1].T, near[1], THREE)
        g10 = g01.T
        upper, lower = [upper[0], lower[0]], [lower[1], upper[1]]
        meets_next = [frozenset((upper[d], lower[d])) for d in range(2)]
        rolled = frozenset((slots[0][0], slots[1][1])) not in meets_next
        if rolled:
            slots[1] = slots[1][::-1]
            g01, g11 = pltpu.roll(g01, h, 1), pltpu.roll(g11, h, 1)
            g10 = jnp.concatenate([g10[h:], g10[:h]], axis=0)
            g11 = jnp.concatenate([g11[h:], g11[:h]], axis=0)
            diagonal[1] = pltpu.roll(diagonal[1], h, 1)
        slots = [[slots[0][0], slots[1][1]], [slots[1][0], slots[0][1]]]

        def mixed(first, second, third, fourth):
            return jnp.concatenate(
                [
                    jnp.where(low_half, first[:h], second[:h]),
                    jnp.where(low_half, third[h:], fourth[h:]),
                ],
                axis=0,
            )

        near = [mixed(g00, g01, g10, g11), mixed(g11, g10, g01, g00)]
        cross = mixed(g01, g00, g11, g10)
        diagonal = [
            jnp.where(cols < h, diagonal[0], diagonal[1]),
            jnp.where(cols < h, diagonal[1], diagonal[0]),
        ]
        if total is None:
            total = [
                jnp.concatenate([factor[0], blank], axis=0),
                jnp.concatenate([blank, factor[1]], axis=0),
            ]
        else:
            total = [long_dot(total[d], factor[d], TWO) for d in range(2)]
        if rolled:
            total[1] = pltpu.roll(total[1], h, 1)
        total = [jnp.where(low, total[0], total[1]), jnp.where(low, total[1], total[0])]

    flat = jnp.concatenate(
        [own_ref[...].reshape(-1, n), other_ref[...].reshape(-1, n)], axis=1
    )
    both = jnp.concatenate(total, axis=1)
    both = jnp.concatenate(
        [jnp.where(side, both[:n], both[n:]), jnp.where(side, both[n:], both[:n])], axis=0
    )
    before_last = long_dot(flat, both, TWO)
    gap = jnp.zeros((n, h), jnp.float32)
    blocks, norms = {}, {}
    for d in range(2):
        norm = jnp.sqrt(diagonal[d][:1])
        for i in range(2):
            part = factor[d][:, i * h : (i + 1) * h]
            blocks[slots[d][i]] = jnp.concatenate([part, gap] if d == 0 else [gap, part], axis=0)
            norms[slots[d][i]] = norm[:, i * h : (i + 1) * h]
    picked = jnp.where(
        side,
        jnp.concatenate([blocks[0], blocks[1]], axis=1),
        jnp.concatenate([blocks[2], blocks[3]], axis=1),
    )
    rotated_ref[...] = long_dot(before_last, picked, TWO).reshape(rotated_ref.shape)
    sigma_ref[...] = jnp.where(
        side,
        jnp.concatenate([norms[0], norms[1]], axis=1),
        jnp.concatenate([norms[2], norms[3]], axis=1),
    )


def shards(snapshots, labels, conductivity, pairing):
    planes, ny, nz, width = snapshots.shape
    cells = planes * ny * nz
    half = width // 2
    count = lax.axis_size("rows")
    swap = [(0, 1), (1, 0)]
    own = snapshots[0]
    labels = labels[0].T
    halo = lax.ppermute(own, "rows", [(i + 2, i) for i in range(count - 2)])
    other = lax.ppermute(own, "cols", swap)
    code = pl.pallas_call(
        code_kernel,
        out_shape=jax.ShapeDtypeStruct((pairing.shape[0] * pairing.shape[1], width), jnp.int32),
        in_specs=[VMEM],
        out_specs=VMEM,
        compiler_params=PARAMS,
    )(pairing)
    beside = lax.ppermute(
        labels,
        ("rows", "cols"),
        [(2 * i, 2 * (i ^ 1)) for i in range(count)]
        + [(2 * i + 1, 2 * (i + (1 if i % 2 else -1)) + 1) for i in range(1, count - 1)],
    )
    gram, turned, own, table = pl.pallas_call(
        local_kernel,
        out_shape=(
            jax.ShapeDtypeStruct((2 * width, width), jnp.float32),
            jax.ShapeDtypeStruct((2 * width, len(THREE) * cells), jnp.bfloat16),
            jax.ShapeDtypeStruct((ny, nz, width), jnp.float32),
            jax.ShapeDtypeStruct((conductivity.shape[0], width), jnp.float32),
        ),
        in_specs=[HBM] * 3 + [VMEM],
        out_specs=[VMEM] * 4,
        scratch_shapes=[
            pltpu.VMEM((cells, width), jnp.float32),
            pltpu.VMEM(labels.shape, jnp.int32),
            pltpu.SMEM(conductivity.shape, jnp.float32),
            pltpu.SemaphoreType.DMA((3,)),
        ],
        compiler_params=PARAMS,
    )(*[pltpu.with_memory_space_constraint(value, pltpu.HBM) for value in (conductivity, own, labels)], other)
    beside, table = lax.optimization_barrier((beside, table))
    across = lax.ppermute(beside, "cols", swap)
    applied, cross, sent = pl.pallas_call(
        functools.partial(halo_kernel, count),
        out_shape=(
            jax.ShapeDtypeStruct((cells, width), jnp.float32),
            jax.ShapeDtypeStruct((half, width), jnp.float32),
            jax.ShapeDtypeStruct((half, width), jnp.float32),
        ),
        in_specs=[VMEM] * 7,
        out_specs=[VMEM] * 3,
        compiler_params=PARAMS,
    )(table, own, halo, beside, across, gram, turned)
    received = lax.ppermute(sent, "cols", swap)
    packed = pl.pallas_call(
        own_kernel,
        out_shape=jax.ShapeDtypeStruct((half + 8, width), jnp.float32),
        in_specs=[VMEM] * 3,
        out_specs=VMEM,
        compiler_params=PARAMS,
    )(gram, turned, applied)
    share = jnp.concatenate([packed, cross + received], axis=0)
    steps = [2**k for k in range(count.bit_length() - 1)]
    for apart in steps[:2][::-1] + steps[2:]:
        share = share + lax.ppermute(share, "rows", [(i, i ^ apart) for i in range(count)])
    theirs = lax.ppermute(share, "cols", swap)
    rotated, sigma = pl.pallas_call(
        functools.partial(tournament_kernel, pairing.shape[0], pairing.shape[1]),
        out_shape=(
            jax.ShapeDtypeStruct((ny, nz, width), jnp.float32),
            jax.ShapeDtypeStruct((1, width), jnp.float32),
        ),
        in_specs=[VMEM] * 5,
        out_specs=[VMEM] * 2,
        compiler_params=PARAMS,
    )(share, theirs, code, own, other)
    return rotated.reshape(snapshots.shape), sigma.reshape(width)


def solution(mesh):
    placed = (
        P(("groups", "rows"), None, None, "cols"),
        P(("groups", "rows"), None, None),
        P("groups"),
        P(),
    )
    return jax.shard_map(
        shards,
        mesh=mesh,
        in_specs=placed,
        out_specs=(P(("groups", "rows"), None, None, "cols"), P(("groups", "cols"))),
        check_vma=False,
    )
```
